256 devices in a mesh: ctx: 32 (over x_lo, z, core), dp: 8 (over y, x_hi).
Axes of the slice: x: 4 (x_hi: 2, x_lo: 2; x = x_hi * 2 + x_lo), y: 4, z: 8, core: 2. Of those that a mesh axis runs over, the one named last changes fastest.
Arguments:
- q_nope: bfloat16 [8, 4096, 2048], P('dp', 'ctx'), may hold values from -8 to 8
- q_rope: bfloat16 [8, 4096, 1024], P('dp', 'ctx'), may hold values from -8 to 8
- dout: bfloat16 [8, 4096, 2048], P('dp', 'ctx'), may hold values from -8 to 8
- latent: bfloat16 [8, 4096, 512], P('dp', 'ctx'), may hold values from -8 to 8
- rope_key: bfloat16 [8, 4096, 64], P('dp', 'ctx'), may hold values from -8 to 8
- doc_ids: int32 [8, 4096], P('dp'), may hold values from 0 to 16, as said below
- w_up: bfloat16 [4096, 512], replicated, may hold values from -0.25 to 0.25
Outputs:
- q_nope_grad: bfloat16 [8, 4096, 2048], P('dp', 'ctx')
- q_rope_grad: bfloat16 [8, 4096, 1024], P('dp', 'ctx')
- latent_grad: float32 [8, 4096, 512], P('dp', 'ctx')
- rope_key_grad: float32 [8, 4096, 64], P('dp', 'ctx')
- up_grad: float32 [4096, 512], P(('ctx', 'dp'))
The draws below stay inside these ranges and needn't reach their ends.
Inputs may be any that keep to these rules, and one draw needn't show every extreme that they name: `doc_ids`: numbers start at 0 at each sequence's first token; each token's number equals its predecessor's or exceeds it by one; every sequence's last number is 16.
All inputs are finite; a program needn't handle non-finite values.
Results may differ from the reference program's by a relative error of at most 0.012.
Values may be sent and summed in bfloat16 or wider, within the bound.
A program may use at most 64 MiB of HBM per device.

```python
import jax
import jax.numpy as jnp
from jax import lax

LATENT = 512
ROPE = 64
HEAD_DIM = 128
HEADS = 16
BLOCK = 128
BAND = 2
SEQS = 8
SEQ_LEN = 4096
N_CTX = 32


def doc_numbers(key):
    start_count = SEQ_LEN // (2 * BLOCK)
    row_keys = jax.random.split(jax.random.fold_in(key, 71), SEQS)
    orders = jax.vmap(lambda one_key: jax.random.permutation(one_key, SEQ_LEN - 1))(row_keys)
    later_starts = (orders < start_count).astype(jnp.int32)
    first_start = jnp.ones((SEQS, 1), jnp.int32)
    starts = jnp.concatenate([first_start, later_starts], axis=1)
    return jnp.cumsum(starts, axis=1) - 1


def draw_doc_ids(key, part):
    return doc_numbers(key).astype(jnp.int32)


def draw_rope_key(key, part):
    own_key = jax.random.fold_in(key, 3)
    values = jnp.clip(jax.random.normal(own_key, (SEQS, SEQ_LEN, ROPE), jnp.float32), -8.0, 8.0)
    return values.astype(jnp.bfloat16)


def draw_q_rope(key, part):
    own_key = jax.random.fold_in(key, 4)
    values = jnp.clip(jax.random.normal(own_key, (SEQS, SEQ_LEN, HEADS * ROPE), jnp.float32), -8.0, 8.0)
    return values.astype(jnp.bfloat16)


def draw_q_nope(key, part):
    own_key = jax.random.fold_in(key, 5)
    values = jnp.clip(jax.random.normal(own_key, (SEQS, SEQ_LEN, HEADS * HEAD_DIM), jnp.float32), -8.0, 8.0)
    return values.astype(jnp.bfloat16)


def shard_levels(rng, shape, cuts, least, high):
    def one(axis_at, blocks):
        steps = jax.random.uniform(jax.random.fold_in(jax.random.fold_in(rng, 6), axis_at), (blocks,), jnp.float32, least / len(cuts), high / len(cuts))
        return jnp.repeat(jnp.exp(steps), shape[axis_at] // blocks).reshape((-1,) + (1,) * (len(shape) - axis_at - 1))

    loudness = one(*cuts[0])
    for cut in cuts[1:]:
        loudness = loudness * one(*cut)
    return loudness


def scatter_about(stream_key, extent, width, limit, shards=(), held_as=jnp.bfloat16):
    gain = shard_levels(stream_key, extent, shards, -0.22, 0.18) if shards else 1.0
    result = jax.random.normal(stream_key, extent, jnp.float32) * width * gain
    return jnp.minimum(jnp.maximum(result, -limit), limit).astype(held_as)


def setup_inputs(seed: int = 0) -> dict:
    key_of = jax.random.split(jax.random.key(seed), 8)
    return {
        "q_nope": draw_q_nope(jax.random.fold_in(key_of[7], 71), 0),
        "q_rope": draw_q_rope(jax.random.fold_in(key_of[7], 71), 0),
        "dout": scatter_about(key_of[2], (SEQS, SEQ_LEN, HEADS * HEAD_DIM), 1.0, 8.0, ((0, 8), (1, 32))),
        "latent": scatter_about(key_of[3], (SEQS, SEQ_LEN, LATENT), 1.0, 8.0, ((0, 8), (1, 32))),
        "rope_key": draw_rope_key(jax.random.fold_in(key_of[7], 71), 0),
        "doc_ids": draw_doc_ids(jax.random.fold_in(key_of[7], 71), 0),
        "w_up": scatter_about(key_of[6], (2 * HEADS * HEAD_DIM, LATENT), LATENT ** -0.5, 0.25),
    }


def attend(query_nope, query_rope, grads_out, keys_values, rope_keys, visible):
    rows_query = query_nope.shape[0]
    rows_key = keys_values.shape[0]
    scale_factor = float(HEAD_DIM + ROPE) ** -0.5
    split_at = HEADS * HEAD_DIM
    queries = query_nope.astype(jnp.float32).reshape(rows_query, HEADS, HEAD_DIM)
    rotary_q = query_rope.astype(jnp.float32).reshape(rows_query, HEADS, ROPE)
    grad_heads = grads_out.astype(jnp.float32).reshape(rows_query, HEADS, HEAD_DIM)
    keys_nope = keys_values[:, :split_at].astype(jnp.float32).reshape(rows_key, HEADS, HEAD_DIM)
    values_all = keys_values[:, split_at:].astype(jnp.float32).reshape(rows_key, HEADS, HEAD_DIM)
    rotary_k = rope_keys.astype(jnp.float32)
    scores = (jnp.einsum('qhd,khd->hqk', queries, keys_nope) + jnp.einsum('qhr,kr->hqk', rotary_q, rotary_k)) * scale_factor
    scores = jnp.where(visible[None], scores, -jnp.inf)
    highest = jnp.max(scores, axis=-1, keepdims=True)
    weights = jnp.exp(scores - highest)
    probs = weights / jnp.sum(weights, axis=-1, keepdims=True)
    probs_low = probs.astype(jnp.bfloat16).astype(jnp.float32)
    outputs = jnp.einsum('hqk,khd->qhd', probs_low, values_all)
    delta = jnp.sum(grad_heads * outputs, axis=-1)
    grad_probs = jnp.einsum('qhd,khd->hqk', grad_heads, values_all)
    grad_scores = (probs * (grad_probs - delta.T[:, :, None]) * scale_factor).astype(jnp.bfloat16).astype(jnp.float32)
    query_grad = jnp.einsum('hqk,khd->qhd', grad_scores, keys_nope).reshape(rows_query, -1)
    rotary_grad = jnp.einsum('hqk,kr->qhr', grad_scores, rotary_k).reshape(rows_query, -1)
    key_grad = jnp.einsum('hqk,qhd->khd', grad_scores, queries).reshape(rows_key, -1)
    value_grad = jnp.einsum('hqk,qhd->khd', probs_low, grad_heads).reshape(rows_key, -1)
    rope_grad = jnp.einsum('hqk,qhr->kr', grad_scores, rotary_q)
    return query_grad, rotary_grad, jnp.concatenate([key_grad, value_grad], axis=1), rope_grad


def reference(q_nope, q_rope, dout, latent, rope_key, doc_ids, w_up):
    weights_wide = w_up.astype(jnp.float32)
    lead_rows = BAND * BLOCK
    span_rows = (BAND + 1) * BLOCK

    def one_sequence(weight_sum, inputs):
        query_row, rotary_row, grad_row, latent_row, rope_row, doc_row = inputs
        keys_all = jnp.dot(latent_row, w_up.T, preferred_element_type=jnp.float32).astype(jnp.bfloat16)
        keys_pad = jnp.concatenate([jnp.zeros((lead_rows, keys_all.shape[1]), jnp.bfloat16), keys_all], axis=0)
        rope_pad = jnp.concatenate([jnp.zeros((lead_rows, ROPE), jnp.bfloat16), rope_row], axis=0)
        doc_pad = jnp.concatenate([jnp.full((lead_rows,), -1, jnp.int32), doc_row.astype(jnp.int32)], axis=0)

        def one_block(state_pair, block_id):
            grad_pad, rope_grad_pad = state_pair
            row_start = (block_id * BLOCK).astype(jnp.int32)
            query_block = lax.dynamic_slice_in_dim(query_row, row_start, BLOCK)
            rotary_block = lax.dynamic_slice_in_dim(rotary_row, row_start, BLOCK)
            grad_block = lax.dynamic_slice_in_dim(grad_row, row_start, BLOCK)
            keys_block = lax.dynamic_slice_in_dim(keys_pad, row_start, span_rows)
            rope_block = lax.dynamic_slice_in_dim(rope_pad, row_start, span_rows)
            query_docs = lax.dynamic_slice_in_dim(doc_row.astype(jnp.int32), row_start, BLOCK)
            key_docs = lax.dynamic_slice_in_dim(doc_pad, row_start, span_rows)
            query_pos = row_start + jnp.arange(BLOCK, dtype=jnp.int32)
            key_pos = row_start - lead_rows + jnp.arange(span_rows, dtype=jnp.int32)
            visible = (key_pos[None, :] <= query_pos[:, None]) & (query_pos[:, None] - key_pos[None, :] < lead_rows) & (query_docs[:, None] == key_docs[None, :])
            query_grad, rotary_grad, key_grad, rope_grad = attend(query_block, rotary_block, grad_block, keys_block, rope_block, visible)
            grad_pad = lax.dynamic_update_slice_in_dim(grad_pad, lax.dynamic_slice_in_dim(grad_pad, row_start, span_rows) + key_grad, row_start, 0)
            rope_grad_pad = lax.dynamic_update_slice_in_dim(rope_grad_pad, lax.dynamic_slice_in_dim(rope_grad_pad, row_start, span_rows) + rope_grad, row_start, 0)
            return (grad_pad, rope_grad_pad), (query_grad.astype(jnp.bfloat16), rotary_grad.astype(jnp.bfloat16))

        start_pair = (jnp.zeros((SEQ_LEN + lead_rows, keys_all.shape[1]), jnp.float32), jnp.zeros((SEQ_LEN + lead_rows, ROPE), jnp.float32))
        final_pair, (query_grads, rotary_grads) = lax.scan(one_block, start_pair, jnp.arange(N_CTX, dtype=jnp.int32))
        grad_keys = final_pair[0][lead_rows:]
        rope_key_grad = final_pair[1][lead_rows:]
        latent_grad = jnp.dot(grad_keys, weights_wide, precision=lax.Precision.HIGHEST)
        weight_sum = weight_sum + lax.dot_general(grad_keys, latent_row.astype(jnp.float32), (((0,), (0,)), ((), ())), precision=lax.Precision.HIGHEST)
        return weight_sum, (query_grads.reshape(SEQ_LEN, -1), rotary_grads.reshape(SEQ_LEN, -1), latent_grad, rope_key_grad)

    start_sum = jnp.zeros((2 * HEADS * HEAD_DIM, LATENT), jnp.float32)
    up_grad, results = lax.scan(one_sequence, start_sum, (q_nope, q_rope, dout, latent, rope_key, doc_ids))
    return results[0], results[1], results[2], results[3], up_grad
```

```python
import functools

import jax
import jax.numpy as jnp
from jax import lax
from jax.experimental import pallas as pl
from jax.experimental.pallas import tpu as pltpu
from jax.sharding import PartitionSpec as P

LATENT = 512
ROPE = 64
DIM = 128
BLOCK = 128
PAIRS = 8
CHIPS = 16
LAG = 2
STEPS = 4
SCALE = float(DIM + ROPE) ** -0.5
LOG2E = 1.4426950408889634
F32 = jnp.float32
BF16 = jnp.bfloat16


def nt(a, b):
    return lax.dot_general(a, b, (((1,), (1,)), ((), ())), preferred_element_type=F32)


def nn(a, b):
    return lax.dot_general(a, b, (((1,), (0,)), ((), ())), preferred_element_type=F32)


def tn(a, b):
    return lax.dot_general(a, b, (((0,), (0,)), ((), ())), preferred_element_type=F32)


def kernel(
    q_nope, q_rope, dout, latent, rope_key, docs, w_up,
    qn_out, qr_out, lat_out, rope_out, up_out,
    lat, ropes, rope_tile, doc_row, bias, w, qd, qg, qr_in, gkv, rope_grad, lgf, lgs, lgr,
    part, in1, out2, in2, total, out3, in3, out4, in4, zf, zb, zin,
    local_sem, head_sem, w_sem, qn_sem,
    lat_send, lat_recv, q_send, q_recv, g_send, g_recv, lg_send, lg_recv,
    rs_send, rs_recv, z_send, z_recv,
):
    ctx = lax.axis_index("ctx")
    dp = lax.axis_index("dp")
    core = lax.rem(ctx, 2)
    other = 1 - core
    chip = lax.div(ctx, 2)
    x_lo, z = lax.div(chip, PAIRS), lax.rem(chip, PAIRS)
    y, x_hi = lax.div(dp, 2), lax.rem(dp, 2)
    y_hi, y_lo = lax.div(y, 2), lax.rem(y, 2)

    def at(ctx_index, dp_index):
        return {"ctx": ctx_index, "dp": dp_index}

    def place(xh, xl, yh, yl, zz):
        return at((xl * PAIRS + zz) * 2 + core, (yh * 2 + yl) * 2 + xh)

    sibling = at(chip * 2 + other, dp)
    after = at(lax.rem(chip + 1, CHIPS) * 2 + core, dp)
    before = at(lax.rem(chip + CHIPS - 1, CHIPS) * 2 + core, dp)
    x_one = place(x_hi, 1 - x_lo, y_hi, y_lo, z)
    x_two = place(1 - x_hi, 1 - x_lo, y_hi, y_lo, z)
    y_one = place(x_hi, x_lo, y_hi, 1 - y_lo, z)
    y_two = place(x_hi, x_lo, 1 - y_hi, 1 - y_lo, z)
    x_p = (lax.rem(x_hi + x_lo, 2), x_hi, x_one, x_two)
    x_q = (x_hi, x_lo, x_two, x_one)
    y_p = (lax.rem(y_hi + y_lo, 2), y_hi, y_one, y_two)
    y_q = (y_hi, y_lo, y_two, y_one)
    first = (x_p, x_q, y_p, y_q)
    second = (y_p, y_q, x_p, x_q)

    own_rows = pl.ds(pl.multiple_of(core * BLOCK, BLOCK), BLOCK)
    sib_rows = pl.ds(pl.multiple_of(other * BLOCK, BLOCK), BLOCK)

    def lat_rows(slot):
        return pl.ds(pl.multiple_of(slot * BLOCK, BLOCK), BLOCK)

    def columns(index):
        return pl.ds(pl.multiple_of(index * DIM, DIM), DIM)

    def remote(src, dst, send, recv, device):
        return pltpu.make_async_remote_copy(
            src_ref=src, dst_ref=dst, send_sem=send, recv_sem=recv,
            device_id=device, device_id_type=pl.DeviceIdType.MESH,
        )

    pltpu.make_async_copy(latent, lat.at[lat_rows(2 + core)], local_sem.at[0]).start()
    pltpu.make_async_copy(rope_key, ropes.at[2 + core], local_sem.at[1]).start()
    behind = lax.rem(chip + CHIPS - 1, CHIPS)
    doc_copies = (
        pltpu.make_async_copy(
            docs.at[:, pl.ds(pl.multiple_of(behind * 256, 256), 256)],
            doc_row.at[:, pl.ds(0, 256)], local_sem.at[2]),
        pltpu.make_async_copy(
            docs.at[:, pl.ds(pl.multiple_of(chip * 256, 256), 256)],
            doc_row.at[:, pl.ds(256, 256)], local_sem.at[3]),
    )
    for copy in doc_copies:
        copy.start()

    def load_head(j, _):
        head = 2 * j + core
        for half in range(2):
            pltpu.make_async_copy(
                w_up.at[half, j, core],
                w.at[pl.ds(pl.multiple_of(j * 256 + half * DIM, DIM), DIM)], w_sem.at[j]).start()
        pltpu.make_async_copy(
            q_nope.at[:, columns(head)], qd.at[j, own_rows, pl.ds(0, DIM)], head_sem.at[j]).start()
        pltpu.make_async_copy(
            q_rope.at[:, columns(j)], qd.at[j, own_rows, pl.ds(DIM, DIM)], head_sem.at[j]).start()
        pltpu.make_async_copy(
            dout.at[:, columns(head)], qd.at[j, own_rows, pl.ds(2 * DIM, DIM)], head_sem.at[j]).start()
        return 0

    lax.fori_loop(0, PAIRS, load_head, 0)

    barrier = pltpu.get_barrier_semaphore()

    def greet(device):
        pl.semaphore_signal(barrier, inc=1, device_id=device, device_id_type=pl.DeviceIdType.MESH)

    for device in (sibling, after, before, x_one, x_two, y_one, y_two):
        greet(device)
    for step in range(1, PAIRS):
        greet(place(x_hi, x_lo, y_hi, y_lo, lax.rem(z + step, PAIRS)))
    pl.semaphore_wait(barrier, 6 + PAIRS)

    lat_next = remote(latent, lat.at[lat_rows(core)], lat_send.at[0], lat_recv.at[0], after)
    rope_next = remote(rope_key, ropes.at[core], lat_send.at[1], lat_recv.at[1], after)
    lat_sib = remote(latent, lat.at[lat_rows(2 + core)], lat_send.at[2], lat_recv.at[2], sibling)
    rope_sib = remote(rope_key, ropes.at[2 + core], lat_send.at[3], lat_recv.at[3], sibling)
    lat_fwd = remote(lat.at[lat_rows(core)], lat.at[lat_rows(core)], lat_send.at[4], lat_recv.at[4], sibling)
    rope_fwd = remote(ropes.at[core], ropes.at[core], lat_send.at[5], lat_recv.at[5], sibling)
    for copy in (lat_next, rope_next, lat_sib, rope_sib):
        copy.start()

    def send_head(j, _):
        head = 2 * j + other
        remote(q_nope.at[:, columns(head)], qd.at[j, own_rows, pl.ds(0, DIM)],
               q_send.at[j], q_recv.at[j], sibling).start()
        remote(q_rope.at[:, columns(j)], qd.at[j, own_rows, pl.ds(DIM, DIM)],
               q_send.at[j], q_recv.at[j], sibling).start()
        remote(dout.at[:, columns(head)], qd.at[j, own_rows, pl.ds(2 * DIM, DIM)],
               q_send.at[j], q_recv.at[j], sibling).start()
        return 0

    lax.fori_loop(0, PAIRS, send_head, 0)

    for copy in doc_copies:
        copy.wait()
    row = doc_row[...].astype(F32)
    key_docs = jnp.transpose(jnp.broadcast_to(row, (DIM, 512)))
    key_docs = jnp.concatenate([key_docs, key_docs], axis=1)
    query_docs = jnp.broadcast_to(row[:, 256:], (512, 256))
    key_at = lax.broadcasted_iota(jnp.int32, (512, 256), 0)
    query_at = lax.broadcasted_iota(jnp.int32, (512, 256), 1)
    first_key = jnp.where(chip == 0, 256, 0)
    seen = (
        (key_at <= query_at + 256) & (key_at > query_at) & (key_at >= first_key)
        & (key_docs == query_docs)
    )
    bias[...] = jnp.where(seen, 0.0, -jnp.inf)
    rope_grad[...] = jnp.zeros_like(rope_grad)

    lat_next.wait_recv()
    lat_fwd.start()
    rope_next.wait_recv()
    rope_fwd.start()
    pltpu.make_async_copy(latent, lat.at[lat_rows(2 + core)], local_sem.at[0]).wait()
    pltpu.make_async_copy(rope_key, ropes.at[2 + core], local_sem.at[1]).wait()
    lat_sib.wait_recv()
    rope_sib.wait_recv()
    lat_fwd.wait_recv()
    rope_fwd.wait_recv()

    spread_row = lax.broadcasted_iota(jnp.int32, (ROPE, DIM), 0)
    spread_col = lax.broadcasted_iota(jnp.int32, (ROPE, DIM), 1)
    spread = jnp.where(spread_col == spread_row + core * ROPE, 1.0, 0.0).astype(BF16)
    for slot in range(4):
        rope_tile[slot * BLOCK:(slot + 1) * BLOCK] = nn(ropes[slot], spread).astype(BF16)

    def attend(j):
        pltpu.make_async_copy(qd.at[j, own_rows], qd.at[j, own_rows], head_sem.at[j]).wait()
        remote(qd.at[j, sib_rows], qd.at[j, sib_rows], q_send.at[j], q_recv.at[j], sibling).wait_recv()
        w_rows = pl.ds(pl.multiple_of(j * 256, 256), 256)
        pltpu.make_async_copy(w.at[w_rows], w.at[w_rows], w_sem.at[j]).wait()
        q_cat = qd[j, :, :256]
        grads = qd[j, :, 256:]
        kv = nt(lat[...], w[w_rows]).astype(BF16)
        k_cat = jnp.concatenate([kv[:, :DIM], rope_tile[...]], axis=1)
        values = kv[:, DIM:]
        scores = nt(k_cat, q_cat) * (SCALE * LOG2E) + bias[...]
        grad_probs = nt(values, grads)
        highest = jnp.max(scores, axis=0, keepdims=True)
        weights = jnp.exp2(scores - highest)
        inverse = 1.0 / jnp.sum(weights, axis=0, keepdims=True)
        probs = weights * inverse
        delta = jnp.sum(probs * grad_probs, axis=0, keepdims=True)
        probs_low = probs.astype(BF16)
        grad_scores = (probs * ((grad_probs - delta) * SCALE)).astype(BF16)
        key_grad = nn(grad_scores, q_cat)
        value_grad = nn(probs_low, grads)
        rope_grad[...] += key_grad[:, DIM:]
        both = jnp.concatenate([key_grad[:, :DIM].astype(BF16), value_grad.astype(BF16)], axis=1)
        gkv[:, pl.ds(pl.multiple_of(j * 256, 256), 256)] = both
        up = tn(both, lat[...]).astype(BF16)
        for xh in range(2):
            for xl in range(2):
                for yy in range(4):
                    yh, yl = yy // 2, yy % 2
                    start = xl * DIM + yy * 32 + xh * 16
                    x_places = ((xh + xl) % 2 * 2 + xh, xh * 2 + xl)
                    y_places = ((yh + yl) % 2 * 2 + yh, yh * 2 + yl)
                    for quarter in range(4):
                        letter = quarter % 2
                        a, b = x_places[letter], y_places[letter]
                        if quarter >= 2:
                            a, b = b, a
                        part[j, quarter, a, b] = up[start:start + 16, quarter * DIM:(quarter + 1) * DIM]
        for quarter in range(4):
            group, _, partner, _ = first[quarter]
            remote(part.at[j, quarter, pl.ds((1 - group) * 2, 2)], in1.at[j, quarter],
                   rs_send.at[0, j], rs_recv.at[0, j], partner).start()
        qg[j] = tn(grad_scores, k_cat).astype(BF16)
        head = 2 * j + core
        remote(qg.at[j, sib_rows, pl.ds(0, DIM)], qn_out.at[:, columns(head)],
               g_send.at[0, j], g_recv.at[0, j], sibling).start()
        remote(qg.at[j, sib_rows, pl.ds(DIM, DIM)], qr_in.at[j],
               g_send.at[1, j], g_recv.at[1, j], sibling).start()
        pltpu.make_async_copy(
            qg.at[j, own_rows, pl.ds(0, DIM)], qn_out.at[:, columns(head)], qn_sem.at[j]).start()

    def arrived(buffer, step, j):
        remote(buffer.at[j], buffer.at[j], rs_send.at[step, j], rs_recv.at[step, j], sibling).wait_recv()

    def step_two(j):
        arrived(in1, 0, j)
        for quarter in range(4):
            group, low, _, partner = first[quarter]
            out2[j, quarter] = (
                part[j, quarter, group * 2 + 1 - low].astype(F32) + in1[j, quarter, 1 - low].astype(F32)
            ).astype(BF16)
            remote(out2.at[j, quarter], in2.at[j, quarter], rs_send.at[1, j], rs_recv.at[1, j], partner).start()

    def step_three(j):
        arrived(in2, 1, j)
        for quarter in range(4):
            group, low, _, _ = first[quarter]
            total[j, quarter] = (
                part[j, quarter, group * 2 + low].astype(F32)
                + in1[j, quarter, low].astype(F32) + in2[j, quarter].astype(F32)
            )
            group, _, partner, _ = second[quarter]
            out3[j, quarter] = total[j, quarter, pl.ds((1 - group) * 2, 2)].astype(BF16)
            remote(out3.at[j, quarter], in3.at[j, quarter], rs_send.at[2, j], rs_recv.at[2, j], partner).start()

    def step_four(j):
        arrived(in3, 2, j)
        for quarter in range(4):
            group, low, _, partner = second[quarter]
            out4[j, quarter] = (
                total[j, quarter, group * 2 + 1 - low] + in3[j, quarter, 1 - low].astype(F32)
            ).astype(BF16)
            remote(out4.at[j, quarter], in4.at[j, quarter], rs_send.at[3, j], rs_recv.at[3, j], partner).start()

    def step_five(j):
        arrived(in4, 3, j)
        for quarter in range(4):
            group, low, _, _ = second[quarter]
            summed = (
                total[j, quarter, group * 2 + low]
                + in3[j, quarter, low].astype(F32) + in4[j, quarter].astype(F32)
            )
            zf[j, :, quarter * DIM:(quarter + 1) * DIM] = summed
            zb[j, :, quarter * DIM:(quarter + 1) * DIM] = summed.astype(BF16)

        @pl.when(j != z)
        def _():
            remote(zb.at[j], zin.at[z], z_send.at[j], z_recv.at[z],
                   place(x_hi, x_lo, y_hi, y_lo, j)).start()

    lg_block = remote(lgs.at[0], lgr.at[0], lg_send.at[0], lg_recv.at[0], sibling)
    lg_own = remote(lgs.at[1], lgr.at[1], lg_send.at[1], lg_recv.at[1], sibling)
    lg_back = remote(lgs.at[2], lgr.at[2], lg_send.at[2], lg_recv.at[2], before)

    def project():
        lane = lax.broadcasted_iota(jnp.int32, (BLOCK, DIM), 1)
        mine = (lane >= core * ROPE) & (lane < (core + 1) * ROPE)
        for slot in range(4):
            rows = slice(slot * BLOCK, (slot + 1) * BLOCK)
            lgf[slot, :, :LATENT] = nn(gkv[rows], w[...])
            lgf[slot, :, LATENT:] = jnp.where(mine, rope_grad[rows], 0.0)
            if slot == 1:
                lgs[0] = lgf[other].astype(BF16)
                lg_block.start()
        lgs[1] = lgf[2 + other].astype(BF16)
        lg_own.start()

    def combine():
        lg_block.wait_recv()
        lgs[2] = (lgf[core] + lgr[0].astype(F32)).astype(BF16)
        lg_back.start()

    def turn(i, _):
        pl.when(i < PAIRS)(lambda: attend(i))
        pl.when(i == PAIRS)(project)
        for number, step in enumerate((step_two, step_three, step_four, step_five)):
            j = i - LAG * (number + 1)
            pl.when((j >= 0) & (j < PAIRS))(functools.partial(step, j))
        pl.when(i == PAIRS)(combine)
        return 0

    lax.fori_loop(0, PAIRS + LAG * STEPS, turn, 0)

    def finish_rope(j, _):
        remote(qr_in.at[j], qr_in.at[j], g_send.at[1, j], g_recv.at[1, j], sibling).wait_recv()
        qr_out[:, columns(j)] = qg[j, own_rows, DIM:] + qr_in[j]
        return 0

    lax.fori_loop(0, PAIRS, finish_rope, 0)
    lg_own.wait_recv()
    lg_back.wait_recv()
    grads = lgf[2 + core] + lgr[1].astype(F32) + lgr[2].astype(F32)
    lat_out[...] = grads[:, :LATENT]
    tile = grads[:, LATENT:]
    rope_out[...] = (tile + pltpu.roll(tile, ROPE, 1))[:, :ROPE]

    up_out[...] = zf[z]

    def add_plane(step, _):
        source = lax.rem(z + step, PAIRS)
        remote(zin.at[source], zin.at[source], z_send.at[source], z_recv.at[source], sibling).wait_recv()
        up_out[...] += zin[source].astype(F32)
        return 0

    lax.fori_loop(1, PAIRS, add_plane, 0)

    for copy in (lat_next, rope_next, lat_sib, rope_sib, lat_fwd, rope_fwd, lg_block, lg_own, lg_back):
        copy.wait_send()

    def ended(j, _):
        remote(qd.at[j, sib_rows], qd.at[j, sib_rows], q_send.at[j], q_recv.at[j], sibling).wait_send()
        head = 2 * j + other
        remote(qg.at[j, sib_rows, pl.ds(0, DIM)], qn_out.at[:, columns(head)],
               g_send.at[0, j], g_recv.at[0, j], sibling).wait()
        remote(qr_in.at[j], qr_in.at[j], g_send.at[1, j], g_recv.at[1, j], sibling).wait_send()
        pltpu.make_async_copy(
            qg.at[j, own_rows, pl.ds(0, DIM)], qn_out.at[:, columns(2 * j + core)], qn_sem.at[j]).wait()
        for step, buffer in enumerate((in1, in2, in3, in4)):
            remote(buffer.at[j], buffer.at[j], rs_send.at[step, j], rs_recv.at[step, j], sibling).wait_send()

        @pl.when(j != z)
        def _():
            remote(zb.at[j], zb.at[j], z_send.at[j], z_recv.at[j], sibling).wait_send()

        return 0

    lax.fori_loop(0, PAIRS, ended, 0)


def fused(q_nope, q_rope, dout, latent, rope_key, docs, w_up):
    any_space = pl.BlockSpec(memory_space=pl.ANY)
    vmem = pl.BlockSpec(memory_space=pltpu.VMEM)
    dma = pltpu.SemaphoreType.DMA
    scratch = [
        pltpu.VMEM((512, LATENT), BF16),
        pltpu.VMEM((4, BLOCK, ROPE), BF16),
        pltpu.VMEM((512, DIM), BF16),
        pltpu.VMEM((1, 512), jnp.int32),
        pltpu.VMEM((512, 256), F32),
        pltpu.VMEM((PAIRS * 256, LATENT), BF16),
        pltpu.VMEM((PAIRS, 256, 3 * DIM), BF16),
        pltpu.VMEM((PAIRS, 256, 256), BF16),
        pltpu.VMEM((PAIRS, BLOCK, DIM), BF16),
        pltpu.VMEM((512, PAIRS * 256), BF16),
        pltpu.VMEM((512, DIM), F32),
        pltpu.VMEM((4, BLOCK, LATENT + DIM), F32),
        pltpu.VMEM((3, BLOCK, LATENT + DIM), BF16),
        pltpu.VMEM((3, BLOCK, LATENT + DIM), BF16),
        pltpu.VMEM((PAIRS, 4, 4, 4, 16, DIM), BF16),
        pltpu.VMEM((PAIRS, 4, 2, 4, 16, DIM), BF16),
        pltpu.VMEM((PAIRS, 4, 4, 16, DIM), BF16),
        pltpu.VMEM((PAIRS, 4, 4, 16, DIM), BF16),
        pltpu.VMEM((PAIRS, 4, 4, 16, DIM), F32),
        pltpu.VMEM((PAIRS, 4, 2, 16, DIM), BF16),
        pltpu.VMEM((PAIRS, 4, 2, 16, DIM), BF16),
        pltpu.VMEM((PAIRS, 4, 16, DIM), BF16),
        pltpu.VMEM((PAIRS, 4, 16, DIM), BF16),
        pltpu.VMEM((PAIRS, 16, LATENT), F32),
        pltpu.VMEM((PAIRS, 16, LATENT), BF16),
        pltpu.VMEM((PAIRS, 16, LATENT), BF16),
        dma((4,)), dma((PAIRS,)), dma((PAIRS,)), dma((PAIRS,)),
        dma((6,)), dma((6,)), dma((PAIRS,)), dma((PAIRS,)),
        dma((2, PAIRS)), dma((2, PAIRS)), dma((3,)), dma((3,)),
        dma((STEPS, PAIRS)), dma((STEPS, PAIRS)), dma((PAIRS,)), dma((PAIRS,)),
    ]
    return pl.pallas_call(
        kernel,
        out_shape=(
            jax.ShapeDtypeStruct((BLOCK, 2048), BF16),
            jax.ShapeDtypeStruct((BLOCK, 1024), BF16),
            jax.ShapeDtypeStruct((BLOCK, LATENT), F32),
            jax.ShapeDtypeStruct((BLOCK, ROPE), F32),
            jax.ShapeDtypeStruct((16, LATENT), F32),
        ),
        in_specs=[any_space] * 7,
        out_specs=(any_space, vmem, vmem, vmem, vmem),
        scratch_shapes=scratch,
        compiler_params=pltpu.CompilerParams(
            collective_id=0, has_side_effects=True, vmem_limit_bytes=48 * 1024 * 1024
        ),
        name="latent_attention_grads",
    )(q_nope, q_rope, dout, latent, rope_key, docs, w_up)


def body(q_nope, q_rope, dout, latent, rope_key, doc_ids, w_up):
    outs = fused(
        q_nope[0], q_rope[0], dout[0], latent[0], rope_key[0], doc_ids,
        w_up.reshape(2, PAIRS, 2, DIM, LATENT),
    )
    return tuple(out[None] for out in outs[:4]) + (outs[4],)


def solution(mesh):
    return jax.shard_map(
        body,
        mesh=mesh,
        in_specs=(
            P("dp", "ctx", None),
            P("dp", "ctx", None),
            P("dp", "ctx", None),
            P("dp", "ctx", None),
            P("dp", "ctx", None),
            P("dp", None),
            P(),
        ),
        out_specs=(
            P("dp", "ctx", None),
            P("dp", "ctx", None),
            P("dp", "ctx", None),
            P("dp", "ctx", None),
            P(("ctx", "dp"), None),
        ),
        check_vma=False,
    )
```

```python
import functools

import jax
import jax.numpy as jnp
from jax import lax
from jax.experimental import pallas as pl
from jax.experimental.pallas import tpu as pltpu
from jax.sharding import PartitionSpec as P

LATENT = 512
ROPE = 64
DIM = 128
BLOCK = 128
PAIRS = 8
CHIPS = 16
CHUNKS = 4
CHUNK = BLOCK // CHUNKS
VMEM_BYTES = 40 * 1024 * 1024
STEPS = 2
SCALE = float(DIM + ROPE) ** -0.5
LOG2E = 1.4426950408889634
F32 = jnp.float32
BF16 = jnp.bfloat16


def nt(a, b):
    return lax.dot_general(a, b, (((1,), (1,)), ((), ())), preferred_element_type=F32)


def nn(a, b):
    return lax.dot_general(a, b, (((1,), (0,)), ((), ())), preferred_element_type=F32)


def tn(a, b):
    return lax.dot_general(a, b, (((0,), (0,)), ((), ())), preferred_element_type=F32)


def offsets(turn):
    late = turn // 2
    return 3 + turn, (1 + 6 * turn) * (1 - late) + (6 - 2 * turn) * late


def kernel(
    q_nope, q_rope, dout, latent, rope_key, docs, w_up,
    qn_out, qr_out, lat_out, rope_out, up_out,
    lat, ropes, rope_tile, doc_row, bias, w, qd, qg, qr_in, gkv, rope_grad, lgf, lgs, lgr,
    kv_own, scores_own, products_own, grad_scores_kept, k_kept, part, in1, total, out2, in2, near_in, zf, zb, zin,
    local_sem, head_sem, w_sem,
    lat_send, lat_recv, q_send, q_recv, g_send, g_recv, lg_send, lg_recv,
    rs_send, rs_recv, z_send, z_recv, near_send, near_recv,
):
    ctx = lax.axis_index("ctx")
    dp = lax.axis_index("dp")
    core = lax.rem(ctx, 2)
    other = 1 - core
    chip = lax.div(ctx, 2)
    x_lo, z = lax.div(chip, PAIRS), lax.rem(chip, PAIRS)
    y, x_hi = lax.div(dp, 2), lax.rem(dp, 2)

    def at(ctx_index, dp_index):
        return {"ctx": ctx_index, "dp": dp_index}

    def place(xh, xl, yy, zz):
        return at((xl * PAIRS + zz) * 2 + core, yy * 2 + xh)

    sibling = at(chip * 2 + other, dp)
    after = at(lax.rem(chip + 1, CHIPS) * 2 + core, dp)
    before = at(lax.rem(chip + CHIPS - 1, CHIPS) * 2 + core, dp)
    x = x_hi * 2 + x_lo

    def x_on(step):
        to = lax.rem(x + step, 4)
        return place(lax.div(to, 2), lax.rem(to, 2), y, z)

    def y_on(step):
        return place(x_hi, x_lo, lax.rem(y + step, 4), z)

    above = place(x_hi, x_lo, y, lax.rem(z + 1, PAIRS))
    below = place(x_hi, x_lo, y, lax.rem(z + PAIRS - 1, PAIRS))
    first = ((x, x_on), (y, y_on))
    second = ((y, y_on), (x, x_on))

    own_rows = pl.ds(pl.multiple_of(core * BLOCK, BLOCK), BLOCK)
    sib_rows = pl.ds(pl.multiple_of(other * BLOCK, BLOCK), BLOCK)

    def lat_rows(slot):
        return pl.ds(pl.multiple_of(slot * BLOCK, BLOCK), BLOCK)

    def columns(index):
        return pl.ds(pl.multiple_of(index * DIM, DIM), DIM)

    def remote(src, dst, send, recv, device):
        return pltpu.make_async_remote_copy(
            src_ref=src, dst_ref=dst, send_sem=send, recv_sem=recv,
            device_id=device, device_id_type=pl.DeviceIdType.MESH,
        )

    barrier = pltpu.get_barrier_semaphore()

    def greet(device):
        pl.semaphore_signal(barrier, inc=1, device_id=device, device_id_type=pl.DeviceIdType.MESH)

    for device in (sibling, after, before):
        greet(device)
    for step in range(1, 4):
        greet(x_on(step))
        greet(y_on(step))
    for step in range(1, PAIRS):
        greet(place(x_hi, x_lo, y, lax.rem(z + step, PAIRS)))

    pltpu.make_async_copy(latent, lat.at[lat_rows(2 + core)], local_sem.at[0]).start()
    pltpu.make_async_copy(rope_key, ropes.at[2 + core], local_sem.at[1]).start()
    behind = lax.rem(chip + CHIPS - 1, CHIPS)
    doc_copies = (
        pltpu.make_async_copy(
            docs.at[:, pl.ds(pl.multiple_of(behind * 256, 256), 256)],
            doc_row.at[:, pl.ds(0, 256)], local_sem.at[2]),
        pltpu.make_async_copy(
            docs.at[:, pl.ds(pl.multiple_of(chip * 256, 256), 256)],
            doc_row.at[:, pl.ds(256, 256)], local_sem.at[3]),
    )
    for copy in doc_copies:
        copy.start()

    def load_head(j, _):
        head = 2 * j + core
        for half in range(2):
            pltpu.make_async_copy(
                w_up.at[half, j, core],
                w.at[pl.ds(pl.multiple_of(j * 256 + half * DIM, DIM), DIM)], w_sem.at[j]).start()
        pltpu.make_async_copy(
            q_nope.at[:, columns(head)], qd.at[j, own_rows, pl.ds(0, DIM)], head_sem.at[j]).start()
        pltpu.make_async_copy(
            q_rope.at[:, columns(j)], qd.at[j, own_rows, pl.ds(DIM, DIM)], head_sem.at[j]).start()
        pltpu.make_async_copy(
            dout.at[:, columns(head)], qd.at[j, own_rows, pl.ds(2 * DIM, DIM)], head_sem.at[j]).start()
        return 0

    lax.fori_loop(0, PAIRS, load_head, 0)

    pl.semaphore_wait(barrier, 8 + PAIRS)


    def lat_chunk(slot, chunk):
        return pl.ds(pl.multiple_of(slot * BLOCK + chunk * CHUNK, CHUNK), CHUNK)

    rope_next = remote(rope_key, ropes.at[core], lat_send.at[0], lat_recv.at[0], after)
    rope_sib = remote(rope_key, ropes.at[2 + core], lat_send.at[1], lat_recv.at[1], sibling)
    rope_fwd = remote(ropes.at[core], ropes.at[core], lat_send.at[2], lat_recv.at[2], sibling)
    lat_sib = remote(latent, lat.at[lat_rows(2 + core)], lat_send.at[3], lat_recv.at[3], sibling)
    lat_next = [
        remote(latent.at[pl.ds(n * CHUNK, CHUNK)], lat.at[lat_chunk(core, n)],
               lat_send.at[4 + n], lat_recv.at[4 + n], after)
        for n in range(CHUNKS)
    ]
    lat_fwd = [
        remote(lat.at[lat_chunk(core, n)], lat.at[lat_chunk(core, n)],
               lat_send.at[4 + CHUNKS + n], lat_recv.at[4 + CHUNKS + n], sibling)
        for n in range(CHUNKS)
    ]
    for copy in (rope_next, *lat_next, lat_sib, rope_sib):
        copy.start()

    def send_head(j, _):
        head = 2 * j + other
        remote(q_nope.at[:, columns(head)], qd.at[j, own_rows, pl.ds(0, DIM)],
               q_send.at[j], q_recv.at[j], sibling).start()
        remote(q_rope.at[:, columns(j)], qd.at[j, own_rows, pl.ds(DIM, DIM)],
               q_send.at[j], q_recv.at[j], sibling).start()
        remote(dout.at[:, columns(head)], qd.at[j, own_rows, pl.ds(2 * DIM, DIM)],
               q_send.at[j], q_recv.at[j], sibling).start()
        return 0

    lax.fori_loop(0, PAIRS, send_head, 0)

    for copy in doc_copies:
        copy.wait()
    row = doc_row[...].astype(F32)
    key_docs = jnp.transpose(jnp.broadcast_to(row, (DIM, 512)))
    key_docs = jnp.concatenate([key_docs, key_docs], axis=1)
    query_docs = jnp.broadcast_to(row[:, 256:], (512, 256))
    key_at = lax.broadcasted_iota(jnp.int32, (512, 256), 0)
    query_at = lax.broadcasted_iota(jnp.int32, (512, 256), 1)
    first_key = jnp.where(chip == 0, 256, 0)
    seen = (
        (key_at <= query_at + 256) & (key_at > query_at) & (key_at >= first_key)
        & (key_docs == query_docs)
    )
    bias[...] = jnp.where(seen, 0.0, -jnp.inf)
    rope_grad[...] = jnp.zeros_like(rope_grad)

    pltpu.make_async_copy(latent, lat.at[lat_rows(2 + core)], local_sem.at[0]).wait()
    pltpu.make_async_copy(rope_key, ropes.at[2 + core], local_sem.at[1]).wait()
    lat_sib.wait_recv()
    rope_sib.wait_recv()

    spread_row = lax.broadcasted_iota(jnp.int32, (ROPE, DIM), 0)
    spread_col = lax.broadcasted_iota(jnp.int32, (ROPE, DIM), 1)
    spread = jnp.where(spread_col == spread_row + core * ROPE, 1.0, 0.0).astype(BF16)

    def spread_rope(slot):
        rope_tile[slot * BLOCK:(slot + 1) * BLOCK] = tn(ropes[slot], spread).astype(BF16)

    spread_rope(2)
    spread_rope(3)

    def wait_weights(j, _):
        w_rows = pl.ds(pl.multiple_of(j * 256, 256), 256)
        pltpu.make_async_copy(w.at[w_rows], w.at[w_rows], w_sem.at[j]).wait()
        return 0

    lax.fori_loop(0, PAIRS, wait_weights, 0)
    kv_own[...] = nt(lat[256:], w[...]).astype(BF16)

    def own_keys(i, _):
        heads = (2 * i, 2 * i + 1)
        for j in heads:
            pltpu.make_async_copy(qd.at[j, own_rows], qd.at[j, own_rows], head_sem.at[j]).wait()
            remote(qd.at[j, sib_rows], qd.at[j, sib_rows], q_send.at[j], q_recv.at[j], sibling).wait_recv()
        kv = kv_own[:, pl.ds(pl.multiple_of(i * 512, 512), 512)]
        rope = rope_tile[256:]
        keys = [jnp.concatenate([kv[:, n * 256:n * 256 + DIM], rope], axis=1) for n in range(2)]
        scores = [nt(keys[n], qd[j, :, :256]) for n, j in enumerate(heads)]
        products = [nt(kv[:, n * 256 + DIM:(n + 1) * 256], qd[j, :, 256:]) for n, j in enumerate(heads)]
        for n, j in enumerate(heads):
            k_kept[j, 256:] = keys[n]
            scores_own[j] = scores[n] * (SCALE * LOG2E) + bias[256:]
            products_own[j] = products[n]
        return 0

    lax.fori_loop(0, PAIRS // 2, own_keys, 0)
    rope_next.wait_recv()
    rope_fwd.start()
    for arriving, onward in zip(lat_next, lat_fwd):
        arriving.wait_recv()
        onward.start()
    rope_fwd.wait_recv()
    for copy in lat_fwd:
        copy.wait_recv()
    spread_rope(0)
    spread_rope(1)

    def pair_on(offset):
        return lax.rem(z + offset, PAIRS)

    def send_first(j):
        for half, (index, on) in enumerate(first):
            for step in range(1, 4):
                remote(part.at[j, half, lax.rem(index + step, 4)], in1.at[j, half, step - 1],
                       rs_send.at[0, j], rs_recv.at[0, j], on(step)).start()

    def attend(i, _):
        heads = [pair_on(offset) for offset in offsets(i)]
        kv = [nt(lat[:256], w[pl.ds(pl.multiple_of(j * 256, 256), 256)]).astype(BF16) for j in heads]
        rope = rope_tile[:256]
        keys = [jnp.concatenate([kv[n][:, :DIM], rope], axis=1) for n in range(2)]
        scores = [nt(keys[n], qd[j, :, :256]) for n, j in enumerate(heads)]
        products = [nt(kv[n][:, DIM:], qd[j, :, 256:]) for n, j in enumerate(heads)]
        probs_low, grad_scores = [], []
        for n, j in enumerate(heads):
            k_kept[j, :256] = keys[n]
            score = jnp.concatenate([scores[n] * (SCALE * LOG2E) + bias[:256], scores_own[j]], axis=0)
            grad_probs = jnp.concatenate([products[n], products_own[j]], axis=0)
            weights = jnp.exp2(score - jnp.max(score, axis=0, keepdims=True))
            probs = weights * (1.0 / jnp.sum(weights, axis=0, keepdims=True))
            delta = jnp.sum(probs * grad_probs, axis=0, keepdims=True)
            probs_low.append(probs.astype(BF16))
            grad_scores.append((probs * ((grad_probs - delta) * SCALE)).astype(BF16))
        rope_sum = rope_grad[...]
        both = []
        for n, j in enumerate(heads):
            key_grad = nn(grad_scores[n], qd[j, :, :256])
            value_grad = nn(probs_low[n], qd[j, :, 256:])
            rope_sum = rope_sum + key_grad[:, DIM:]
            both.append(jnp.concatenate([key_grad[:, :DIM].astype(BF16), value_grad.astype(BF16)], axis=1))
        rope_grad[...] = rope_sum
        for n, j in enumerate(heads):
            gkv[:, pl.ds(pl.multiple_of(j * 256, 256), 256)] = both[n]
        ups = [tn(both[n], lat[...]).astype(BF16) for n in range(2)]
        for n, j in enumerate(heads):
            for to_x in range(4):
                for to_y in range(4):
                    start = to_x % 2 * DIM + to_y * 32 + to_x // 2 * 16
                    part[j, 0, to_x, to_y] = ups[n][start:start + 16, :256]
                    part[j, 1, to_y, to_x] = ups[n][start:start + 16, 256:]
        send_first(heads[0])
        pl.when(i == 0)(lambda: remote(
            part.at[heads[1]], near_in.at[0], near_send.at[0], near_recv.at[0], above).start())
        pl.when(i == 1)(lambda: remote(
            part.at[heads[1]], near_in.at[1], near_send.at[1], near_recv.at[1], below).start())
        pl.when(i == 2)(lambda: send_first(heads[1]))
        for n, j in enumerate(heads):
            grad_scores_kept[j] = grad_scores[n]
        return 0

    def merge_near():
        for n, device in enumerate((above, below)):
            remote(near_in.at[n], near_in.at[n], near_send.at[n], near_recv.at[n], device).wait_recv()

        def merge_part(index, _):
            for half in range(2):
                part[z, half, index] = (
                    part[z, half, index].astype(F32)
                    + near_in[0, half, index].astype(F32) + near_in[1, half, index].astype(F32)
                ).astype(BF16)
            return 0

        lax.fori_loop(0, 4, merge_part, 0)
        send_first(z)

    def query_grads(i, _):
        heads = (2 * i, 2 * i + 1)
        grads = [tn(grad_scores_kept[j], k_kept[j]).astype(BF16) for j in heads]
        for n, j in enumerate(heads):
            qg[j] = grads[n]
            head = 2 * j + core
            remote(qg.at[j, sib_rows, pl.ds(0, DIM)], qn_out.at[:, columns(head)],
                   g_send.at[0, j], g_recv.at[0, j], sibling).start()
            remote(qg.at[j, sib_rows, pl.ds(DIM, DIM)], qr_in.at[j],
                   g_send.at[1, j], g_recv.at[1, j], sibling).start()
            qn_out[:, columns(head)] = qg[j, own_rows, :DIM]
        return 0

    def arrived(buffer, step, j):
        remote(buffer.at[j], buffer.at[j], rs_send.at[step, j], rs_recv.at[step, j], sibling).wait_recv()

    def step_two(j):
        arrived(in1, 0, j)
        for half, (index, on) in enumerate(second):
            own, _ = first[half]
            summed = part[j, half, own].astype(F32)
            for step in range(3):
                summed = summed + in1[j, half, step].astype(F32)
            total[j, half] = summed
            out2[j, half] = summed.astype(BF16)
            for step in range(1, 4):
                remote(out2.at[j, half, lax.rem(index + step, 4)], in2.at[j, half, step - 1],
                       rs_send.at[1, j], rs_recv.at[1, j], on(step)).start()

    def step_three(j):
        arrived(in2, 1, j)
        for half, (own, _) in enumerate(second):
            summed = total[j, half, own]
            for step in range(3):
                summed = summed + in2[j, half, step].astype(F32)
            zf[j, :, half * 256:(half + 1) * 256] = summed
            zb[j, :, half * 256:(half + 1) * 256] = summed.astype(BF16)

    def step_four(j):
        remote(zb.at[j], zin.at[z], z_send.at[j], z_recv.at[z], place(x_hi, x_lo, y, j)).start()

    lg_block = remote(lgs.at[0], lgr.at[0], lg_send.at[0], lg_recv.at[0], sibling)
    lg_own = remote(lgs.at[1], lgr.at[1], lg_send.at[1], lg_recv.at[1], sibling)
    lg_back = remote(lgs.at[2], lgr.at[2], lg_send.at[2], lg_recv.at[2], before)

    def project():
        lane = lax.broadcasted_iota(jnp.int32, (BLOCK, DIM), 1)
        mine = (lane >= core * ROPE) & (lane < (core + 1) * ROPE)
        for slot in range(4):
            rows = slice(slot * BLOCK, (slot + 1) * BLOCK)
            lgf[slot, :, :LATENT] = nn(gkv[rows], w[...])
            lgf[slot, :, LATENT:] = jnp.where(mine, rope_grad[rows], 0.0)
            if slot == 1:
                lgs[0] = lgf[other].astype(BF16)
                lg_block.start()
        lgs[1] = lgf[2 + other].astype(BF16)
        lg_own.start()

    def combine():
        lg_block.wait_recv()
        lgs[2] = (lgf[core] + lgr[0].astype(F32)).astype(BF16)
        lg_back.start()

    def finish_plane(offset):
        step_three(pair_on(offset))
        step_four(pair_on(offset))

    lax.fori_loop(0, PAIRS // 2, attend, 0)
    step_two(pair_on(3))
    project()
    step_two(pair_on(4))
    lax.fori_loop(0, 2, query_grads, 0)
    combine()
    step_two(pair_on(5))
    finish_plane(3)
    lax.fori_loop(2, 4, query_grads, 0)
    step_two(pair_on(2))
    merge_near()
    finish_plane(4)
    step_two(pair_on(6))
    finish_plane(5)
    finish_plane(2)

    def finish_head(j, _):
        head = 2 * j + other
        remote(qg.at[j, sib_rows, pl.ds(0, DIM)], qn_out.at[:, columns(head)],
               g_send.at[0, j], g_recv.at[0, j], sibling).wait()
        remote(qr_in.at[j], qr_in.at[j], g_send.at[1, j], g_recv.at[1, j], sibling).wait()
        qr_out[:, columns(j)] = qg[j, own_rows, DIM:] + qr_in[j]
        remote(qd.at[j, sib_rows], qd.at[j, sib_rows], q_send.at[j], q_recv.at[j], sibling).wait_send()
        return 0

    lax.fori_loop(0, PAIRS, finish_head, 0)
    for n, device in enumerate((above, below)):
        remote(near_in.at[n], near_in.at[n], near_send.at[n], near_recv.at[n], device).wait_send()
    lg_own.wait_recv()
    lg_back.wait_recv()
    grads = lgf[2 + core] + lgr[1].astype(F32) + lgr[2].astype(F32)
    lat_out[...] = grads[:, :LATENT]
    tile = grads[:, LATENT:]
    rope_out[...] = jnp.transpose(tile + pltpu.roll(tile, ROPE, 1))[:ROPE]
    for copy in (rope_next, *lat_next, lat_sib, rope_sib, *lat_fwd, rope_fwd, lg_block, lg_own, lg_back):
        copy.wait_send()

    step_two(z)
    finish_plane(6)
    step_three(z)
    up_out[...] = zf[z]

    def add_plane(step, _):
        source = lax.rem(z + step, PAIRS)
        remote(zin.at[source], zin.at[source], z_send.at[source], z_recv.at[source], sibling).wait_recv()
        up_out[...] += zin[source].astype(F32)
        return 0

    lax.fori_loop(2, PAIRS - 1, add_plane, 0)

    def sums_ended(step, _):
        j = pair_on(step)
        for number, buffer in enumerate((in1, in2)):
            remote(buffer.at[j], buffer.at[j], rs_send.at[number, j], rs_recv.at[number, j], sibling).wait_send()
        return 0

    def plane_ended(step, _):
        j = pair_on(step)
        remote(zb.at[j], zb.at[j], z_send.at[j], z_recv.at[j], sibling).wait_send()
        return sums_ended(step, 0)

    lax.fori_loop(2, PAIRS - 1, plane_ended, 0)
    sums_ended(0, 0)


def fused(*arrays):
    hbm = pl.BlockSpec(memory_space=pltpu.HBM)
    dma = pltpu.SemaphoreType.DMA
    scratch = [
        pltpu.VMEM((512, LATENT), BF16),
        pltpu.VMEM((4, ROPE, BLOCK), BF16),
        pltpu.VMEM((512, DIM), BF16),
        pltpu.VMEM((1, 512), jnp.int32),
        pltpu.VMEM((512, 256), F32),
        pltpu.VMEM((PAIRS * 256, LATENT), BF16),
        pltpu.VMEM((PAIRS, 256, 3 * DIM), BF16),
        pltpu.VMEM((PAIRS, 256, 256), BF16),
        pltpu.VMEM((PAIRS, BLOCK, DIM), BF16),
        pltpu.VMEM((512, PAIRS * 256), BF16),
        pltpu.VMEM((512, DIM), F32),
        pltpu.VMEM((4, BLOCK, LATENT + DIM), F32),
        pltpu.VMEM((3, BLOCK, LATENT + DIM), BF16),
        pltpu.VMEM((3, BLOCK, LATENT + DIM), BF16),
        pltpu.VMEM((256, PAIRS * 256), BF16),
        pltpu.VMEM((PAIRS, 256, 256), F32),
        pltpu.VMEM((PAIRS, 256, 256), F32),
        pltpu.VMEM((PAIRS, 512, 256), BF16),
        pltpu.VMEM((PAIRS, 512, 256), BF16),
        pltpu.VMEM((PAIRS, 2, 4, 4, 16, 256), BF16),
        pltpu.VMEM((PAIRS, 2, 3, 4, 16, 256), BF16),
        pltpu.VMEM((PAIRS, 2, 4, 16, 256), F32),
        pltpu.VMEM((PAIRS, 2, 4, 16, 256), BF16),
        pltpu.VMEM((PAIRS, 2, 3, 16, 256), BF16),
        pltpu.VMEM((2, 2, 4, 4, 16, 256), BF16),
        pltpu.VMEM((PAIRS, 16, LATENT), F32),
        pltpu.VMEM((PAIRS, 16, LATENT), BF16),
        pltpu.VMEM((PAIRS, 16, LATENT), BF16),
        dma((4,)), dma((PAIRS,)), dma((PAIRS,)),
        dma((4 + 2 * CHUNKS,)), dma((4 + 2 * CHUNKS,)), dma((PAIRS,)), dma((PAIRS,)),
        dma((2, PAIRS)), dma((2, PAIRS)), dma((3,)), dma((3,)),
        dma((STEPS, PAIRS)), dma((STEPS, PAIRS)), dma((PAIRS,)), dma((PAIRS,)), dma((2,)), dma((2,)),
    ]
    return pl.pallas_call(
        kernel,
        out_shape=(
            jax.ShapeDtypeStruct((BLOCK, 2048), BF16),
            jax.ShapeDtypeStruct((BLOCK, 1024), BF16),
            jax.ShapeDtypeStruct((BLOCK, LATENT), F32),
            jax.ShapeDtypeStruct((ROPE, BLOCK), F32),
            jax.ShapeDtypeStruct((16, LATENT), F32),
        ),
        in_specs=[hbm] * 7,
        out_specs=(pl.BlockSpec(memory_space=pltpu.VMEM),) * 5,
        scratch_shapes=scratch,
        compiler_params=pltpu.CompilerParams(
            collective_id=0, has_side_effects=True, vmem_limit_bytes=VMEM_BYTES
        ),
        name="latent_attention_grads",
    )(*(pltpu.with_memory_space_constraint(a, pltpu.HBM) for a in arrays))


def write_kernel(count, *refs):
    sources, targets, sems = refs[:count], refs[count:2 * count], refs[2 * count]
    copies = [pltpu.make_async_copy(sources[n], targets[n], sems.at[n]) for n in range(count)]
    for copy in copies:
        copy.start()
    for copy in copies:
        copy.wait()


def write(values):
    count = len(values)
    return pl.pallas_call(
        functools.partial(write_kernel, count),
        out_shape=tuple(jax.ShapeDtypeStruct(value.shape, value.dtype) for value in values),
        in_specs=[pl.BlockSpec(memory_space=pltpu.VMEM)] * count,
        out_specs=(pl.BlockSpec(memory_space=pltpu.HBM),) * count,
        scratch_shapes=[pltpu.SemaphoreType.DMA((count,))],
        name="write_results",
    )(*(pltpu.with_memory_space_constraint(v, pltpu.VMEM) for v in values))


def body(q_nope, q_rope, dout, latent, rope_key, doc_ids, w_up):
    outs = write(fused(
        q_nope[0], q_rope[0], dout[0], latent[0], rope_key[0].T, doc_ids,
        w_up.reshape(2, PAIRS, 2, DIM, LATENT),
    ))
    return (outs[0][None], outs[1][None], outs[2][None], outs[3].T[None], outs[4])


def solution(mesh):
    return jax.shard_map(
        body,
        mesh=mesh,
        in_specs=(
            P("dp", "ctx", None),
            P("dp", "ctx", None),
            P("dp", "ctx", None),
            P("dp", "ctx", None),
            P("dp", "ctx", None),
            P("dp", None),
            P(),
        ),
        out_specs=(
            P("dp", "ctx", None),
            P("dp", "ctx", None),
            P("dp", "ctx", None),
            P("dp", "ctx", None),
            P(("ctx", "dp"), None),
        ),
        check_vma=False,
    )
```

```python
import functools

import jax
import jax.numpy as jnp
from jax import lax
from jax.experimental import pallas as pl
from jax.experimental.pallas import tpu as pltpu
from jax.sharding import PartitionSpec as P

LATENT = 512
ROPE = 64
DIM = 128
BLOCK = 128
PAIRS = 8
CHIPS = 16
CHUNKS = 4
CHUNK = BLOCK // CHUNKS
VMEM_BYTES = 40 * 1024 * 1024
STEPS = 2
SCALE = float(DIM + ROPE) ** -0.5
LOG2E = 1.4426950408889634
F32 = jnp.float32
BF16 = jnp.bfloat16


def nt(a, b):
    return lax.dot_general(a, b, (((1,), (1,)), ((), ())), preferred_element_type=F32)


def nn(a, b):
    return lax.dot_general(a, b, (((1,), (0,)), ((), ())), preferred_element_type=F32)


def tn(a, b):
    return lax.dot_general(a, b, (((0,), (0,)), ((), ())), preferred_element_type=F32)


def offsets(turn):
    late = turn // 2
    return 3 + turn, (1 + 6 * turn) * (1 - late) + (6 - 2 * turn) * late


def kernel(
    q_nope, q_rope, dout, latent, rope_key, docs, w_up,
    qn_out, qr_out, lat_out, rope_out, up_out,
    lat, ropes, rope_tile, doc_row, bias, w, qd, qg, qr_in, gkv, rope_grad, lgf, lgs, lgr,
    kv_own, scores_own, products_own, grad_scores_kept, k_kept, part, in1, total, out2, in2, near_in, zf, zb, zin,
    local_sem, head_sem, w_sem,
    lat_send, lat_recv, q_send, q_recv, g_send, g_recv, lg_send, lg_recv,
    rs_send, rs_recv, z_send, z_recv, near_send, near_recv,
):
    ctx = lax.axis_index("ctx")
    dp = lax.axis_index("dp")
    core = lax.rem(ctx, 2)
    other = 1 - core
    chip = lax.div(ctx, 2)
    x_lo, z = lax.div(chip, PAIRS), lax.rem(chip, PAIRS)
    y, x_hi = lax.div(dp, 2), lax.rem(dp, 2)

    def at(ctx_index, dp_index):
        return {"ctx": ctx_index, "dp": dp_index}

    def place(xh, xl, yy, zz):
        return at((xl * PAIRS + zz) * 2 + core, yy * 2 + xh)

    sibling = at(chip * 2 + other, dp)
    after = at(lax.rem(chip + 1, CHIPS) * 2 + core, dp)
    before = at(lax.rem(chip + CHIPS - 1, CHIPS) * 2 + core, dp)
    x = x_hi * 2 + x_lo

    def x_on(step):
        to = lax.rem(x + step, 4)
        return place(lax.div(to, 2), lax.rem(to, 2), y, z)

    def y_on(step):
        return place(x_hi, x_lo, lax.rem(y + step, 4), z)

    above = place(x_hi, x_lo, y, lax.rem(z + 1, PAIRS))
    below = place(x_hi, x_lo, y, lax.rem(z + PAIRS - 1, PAIRS))
    first = ((x, x_on), (y, y_on))
    second = ((y, y_on), (x, x_on))

    own_rows = pl.ds(pl.multiple_of(core * BLOCK, BLOCK), BLOCK)
    sib_rows = pl.ds(pl.multiple_of(other * BLOCK, BLOCK), BLOCK)

    def lat_rows(slot):
        return pl.ds(pl.multiple_of(slot * BLOCK, BLOCK), BLOCK)

    def columns(index):
        return pl.ds(pl.multiple_of(index * DIM, DIM), DIM)

    def remote(src, dst, send, recv, device):
        return pltpu.make_async_remote_copy(
            src_ref=src, dst_ref=dst, send_sem=send, recv_sem=recv,
            device_id=device, device_id_type=pl.DeviceIdType.MESH,
        )

    barrier = pltpu.get_barrier_semaphore()

    def greet(device):
        pl.semaphore_signal(barrier, inc=1, device_id=device, device_id_type=pl.DeviceIdType.MESH)

    for device in (sibling, after, before):
        greet(device)
    for step in range(1, 4):
        greet(x_on(step))
        greet(y_on(step))
    for step in range(1, PAIRS):
        greet(place(x_hi, x_lo, y, lax.rem(z + step, PAIRS)))

    pltpu.make_async_copy(latent, lat.at[lat_rows(2 + core)], local_sem.at[0]).start()
    pltpu.make_async_copy(rope_key, ropes.at[2 + core], local_sem.at[1]).start()
    behind = lax.rem(chip + CHIPS - 1, CHIPS)
    doc_copies = (
        pltpu.make_async_copy(
            docs.at[:, pl.ds(pl.multiple_of(behind * 256, 256), 256)],
            doc_row.at[:, pl.ds(0, 256)], local_sem.at[2]),
        pltpu.make_async_copy(
            docs.at[:, pl.ds(pl.multiple_of(chip * 256, 256), 256)],
            doc_row.at[:, pl.ds(256, 256)], local_sem.at[3]),
    )
    for copy in doc_copies:
        copy.start()

    def load_head(j, _):
        head = 2 * j + core
        for half in range(2):
            pltpu.make_async_copy(
                w_up.at[half, j, core],
                w.at[pl.ds(pl.multiple_of(j * 256 + half * DIM, DIM), DIM)], w_sem.at[j]).start()
        pltpu.make_async_copy(
            q_nope.at[:, columns(head)], qd.at[j, own_rows, pl.ds(0, DIM)], head_sem.at[j]).start()
        pltpu.make_async_copy(
            q_rope.at[:, columns(j)], qd.at[j, own_rows, pl.ds(DIM, DIM)], head_sem.at[j]).start()
        pltpu.make_async_copy(
            dout.at[:, columns(head)], qd.at[j, own_rows, pl.ds(2 * DIM, DIM)], head_sem.at[j]).start()
        return 0

    lax.fori_loop(0, PAIRS, load_head, 0)

    pl.semaphore_wait(barrier, 8 + PAIRS)


    def lat_chunk(slot, chunk):
        return pl.ds(pl.multiple_of(slot * BLOCK + chunk * CHUNK, CHUNK), CHUNK)

    rope_next = remote(rope_key, ropes.at[core], lat_send.at[0], lat_recv.at[0], after)
    rope_sib = remote(rope_key, ropes.at[2 + core], lat_send.at[1], lat_recv.at[1], sibling)
    rope_fwd = remote(ropes.at[core], ropes.at[core], lat_send.at[2], lat_recv.at[2], sibling)
    lat_sib = remote(latent, lat.at[lat_rows(2 + core)], lat_send.at[3], lat_recv.at[3], sibling)
    lat_next = [
        remote(latent.at[pl.ds(n * CHUNK, CHUNK)], lat.at[lat_chunk(core, n)],
               lat_send.at[4 + n], lat_recv.at[4 + n], after)
        for n in range(CHUNKS)
    ]
    lat_fwd = [
        remote(lat.at[lat_chunk(core, n)], lat.at[lat_chunk(core, n)],
               lat_send.at[4 + CHUNKS + n], lat_recv.at[4 + CHUNKS + n], sibling)
        for n in range(CHUNKS)
    ]
    for copy in (rope_next, *lat_next, lat_sib, rope_sib):
        copy.start()

    def send_head(j, _):
        head = 2 * j + other
        remote(q_nope.at[:, columns(head)], qd.at[j, own_rows, pl.ds(0, DIM)],
               q_send.at[j], q_recv.at[j], sibling).start()
        remote(q_rope.at[:, columns(j)], qd.at[j, own_rows, pl.ds(DIM, DIM)],
               q_send.at[j], q_recv.at[j], sibling).start()
        remote(dout.at[:, columns(head)], qd.at[j, own_rows, pl.ds(2 * DIM, DIM)],
               q_send.at[j], q_recv.at[j], sibling).start()
        return 0

    lax.fori_loop(0, PAIRS, send_head, 0)

    for copy in doc_copies:
        copy.wait()
    row = doc_row[...].astype(F32)
    key_docs = jnp.transpose(jnp.broadcast_to(row, (DIM, 512)))
    key_docs = jnp.concatenate([key_docs, key_docs], axis=1)
    query_docs = jnp.broadcast_to(row[:, 256:], (512, 256))
    key_at = lax.broadcasted_iota(jnp.int32, (512, 256), 0)
    query_at = lax.broadcasted_iota(jnp.int32, (512, 256), 1)
    first_key = jnp.where(chip == 0, 256, 0)
    seen = (
        (key_at <= query_at + 256) & (key_at > query_at) & (key_at >= first_key)
        & (key_docs == query_docs)
    )
    bias[...] = jnp.where(seen, 0.0, -jnp.inf)
    rope_grad[...] = jnp.zeros_like(rope_grad)

    pltpu.make_async_copy(latent, lat.at[lat_rows(2 + core)], local_sem.at[0]).wait()
    pltpu.make_async_copy(rope_key, ropes.at[2 + core], local_sem.at[1]).wait()
    lat_sib.wait_recv()
    rope_sib.wait_recv()

    spread_row = lax.broadcasted_iota(jnp.int32, (ROPE, DIM), 0)
    spread_col = lax.broadcasted_iota(jnp.int32, (ROPE, DIM), 1)
    spread = jnp.where(spread_col == spread_row + core * ROPE, 1.0, 0.0).astype(BF16)

    def spread_rope(slot):
        rope_tile[slot * BLOCK:(slot + 1) * BLOCK] = tn(ropes[slot], spread).astype(BF16)

    spread_rope(2)
    spread_rope(3)

    def wait_weights(j, _):
        w_rows = pl.ds(pl.multiple_of(j * 256, 256), 256)
        pltpu.make_async_copy(w.at[w_rows], w.at[w_rows], w_sem.at[j]).wait()
        return 0

    lax.fori_loop(0, PAIRS, wait_weights, 0)
    kv_own[...] = nt(lat[256:], w[...]).astype(BF16)

    def own_keys(i, _):
        heads = (2 * i, 2 * i + 1)
        for j in heads:
            pltpu.make_async_copy(qd.at[j, own_rows], qd.at[j, own_rows], head_sem.at[j]).wait()
            remote(qd.at[j, sib_rows], qd.at[j, sib_rows], q_send.at[j], q_recv.at[j], sibling).wait_recv()
        kv = kv_own[:, pl.ds(pl.multiple_of(i * 512, 512), 512)]
        rope = rope_tile[256:]
        keys = [jnp.concatenate([kv[:, n * 256:n * 256 + DIM], rope], axis=1) for n in range(2)]
        scores = [nt(keys[n], qd[j, :, :256]) for n, j in enumerate(heads)]
        products = [nt(kv[:, n * 256 + DIM:(n + 1) * 256], qd[j, :, 256:]) for n, j in enumerate(heads)]
        for n, j in enumerate(heads):
            k_kept[j, 256:] = keys[n]
            scores_own[j] = scores[n] * (SCALE * LOG2E) + bias[256:]
            products_own[j] = products[n]
        return 0

    lax.fori_loop(0, PAIRS // 2, own_keys, 0)
    rope_next.wait_recv()
    rope_fwd.start()
    for arriving, onward in zip(lat_next, lat_fwd):
        arriving.wait_recv()
        onward.start()
    rope_fwd.wait_recv()
    spread_rope(0)
    spread_rope(1)
    for copy in lat_fwd:
        copy.wait_recv()

    def pair_on(offset):
        return lax.rem(z + offset, PAIRS)

    def send_first(j):
        for half, (index, on) in enumerate(first):
            for step in range(1, 4):
                remote(part.at[j, half, lax.rem(index + step, 4)], in1.at[j, half, step - 1],
                       rs_send.at[0, j], rs_recv.at[0, j], on(step)).start()

    def attend(i, _):
        heads = [pair_on(offset) for offset in offsets(i)]
        kv = [nt(lat[:256], w[pl.ds(pl.multiple_of(j * 256, 256), 256)]).astype(BF16) for j in heads]
        rope = rope_tile[:256]
        keys = [jnp.concatenate([kv[n][:, :DIM], rope], axis=1) for n in range(2)]
        scores = [nt(keys[n], qd[j, :, :256]) for n, j in enumerate(heads)]
        products = [nt(kv[n][:, DIM:], qd[j, :, 256:]) for n, j in enumerate(heads)]
        probs_low, grad_scores = [], []
        for n, j in enumerate(heads):
            k_kept[j, :256] = keys[n]
            score = jnp.concatenate([scores[n] * (SCALE * LOG2E) + bias[:256], scores_own[j]], axis=0)
            grad_probs = jnp.concatenate([products[n], products_own[j]], axis=0)
            weights = jnp.exp2(score - jnp.max(score, axis=0, keepdims=True))
            probs = weights * (1.0 / jnp.sum(weights, axis=0, keepdims=True))
            delta = jnp.sum(probs * grad_probs, axis=0, keepdims=True)
            probs_low.append(probs.astype(BF16))
            grad_scores.append((probs * ((grad_probs - delta) * SCALE)).astype(BF16))
        rope_sum = rope_grad[...]
        both = []
        for n, j in enumerate(heads):
            key_grad = nn(grad_scores[n], qd[j, :, :256])
            value_grad = nn(probs_low[n], qd[j, :, 256:])
            rope_sum = rope_sum + key_grad[:, DIM:]
            both.append(jnp.concatenate([key_grad[:, :DIM].astype(BF16), value_grad.astype(BF16)], axis=1))
        rope_grad[...] = rope_sum
        for n, j in enumerate(heads):
            gkv[:, pl.ds(pl.multiple_of(j * 256, 256), 256)] = both[n]
        ups = [tn(both[n], lat[...]).astype(BF16) for n in range(2)]
        for n, j in enumerate(heads):
            for to_x in range(4):
                for to_y in range(4):
                    start = to_x % 2 * DIM + to_y * 32 + to_x // 2 * 16
                    part[j, 0, to_x, to_y] = ups[n][start:start + 16, :256]
                    part[j, 1, to_y, to_x] = ups[n][start:start + 16, 256:]
        send_first(heads[0])
        pl.when(i == 0)(lambda: remote(
            part.at[heads[1]], near_in.at[0], near_send.at[0], near_recv.at[0], above).start())
        pl.when(i == 1)(lambda: remote(
            part.at[heads[1]], near_in.at[1], near_send.at[1], near_recv.at[1], below).start())
        pl.when(i == 2)(lambda: send_first(heads[1]))
        for n, j in enumerate(heads):
            grad_scores_kept[j] = grad_scores[n]
        return 0

    def merge_near():
        for n, device in enumerate((above, below)):
            remote(near_in.at[n], near_in.at[n], near_send.at[n], near_recv.at[n], device).wait_recv()

        def merge_part(index, _):
            for half in range(2):
                part[z, half, index] = (
                    part[z, half, index].astype(F32)
                    + near_in[0, half, index].astype(F32) + near_in[1, half, index].astype(F32)
                ).astype(BF16)
            return 0

        lax.fori_loop(0, 4, merge_part, 0)
        send_first(z)

    def query_grads(i, _):
        heads = (2 * i, 2 * i + 1)
        grads = [tn(grad_scores_kept[j], k_kept[j]).astype(BF16) for j in heads]
        for n, j in enumerate(heads):
            qg[j] = grads[n]
            head = 2 * j + core
            remote(qg.at[j, sib_rows, pl.ds(0, DIM)], qn_out.at[:, columns(head)],
                   g_send.at[0, j], g_recv.at[0, j], sibling).start()
            remote(qg.at[j, sib_rows, pl.ds(DIM, DIM)], qr_in.at[j],
                   g_send.at[1, j], g_recv.at[1, j], sibling).start()
            qn_out[:, columns(head)] = qg[j, own_rows, :DIM]
        return 0

    def arrived(buffer, step, j):
        remote(buffer.at[j], buffer.at[j], rs_send.at[step, j], rs_recv.at[step, j], sibling).wait_recv()

    def step_two(j):
        arrived(in1, 0, j)
        for half, (index, on) in enumerate(second):
            own, _ = first[half]
            summed = part[j, half, own].astype(F32)
            for step in range(3):
                summed = summed + in1[j, half, step].astype(F32)
            total[j, half] = summed
            out2[j, half] = summed.astype(BF16)
            for step in range(1, 4):
                remote(out2.at[j, half, lax.rem(index + step, 4)], in2.at[j, half, step - 1],
                       rs_send.at[1, j], rs_recv.at[1, j], on(step)).start()

    def step_three(j):
        arrived(in2, 1, j)
        for half, (own, _) in enumerate(second):
            summed = total[j, half, own]
            for step in range(3):
                summed = summed + in2[j, half, step].astype(F32)
            zf[j, :, half * 256:(half + 1) * 256] = summed
            zb[j, :, half * 256:(half + 1) * 256] = summed.astype(BF16)

    def step_four(j):
        remote(zb.at[j], zin.at[z], z_send.at[j], z_recv.at[z], place(x_hi, x_lo, y, j)).start()

    lg_block = remote(lgs.at[0], lgr.at[0], lg_send.at[0], lg_recv.at[0], sibling)
    lg_own = remote(lgs.at[1], lgr.at[1], lg_send.at[1], lg_recv.at[1], sibling)
    lg_back = remote(lgs.at[2], lgr.at[2], lg_send.at[2], lg_recv.at[2], before)

    def project():
        lane = lax.broadcasted_iota(jnp.int32, (BLOCK, DIM), 1)
        mine = (lane >= core * ROPE) & (lane < (core + 1) * ROPE)
        for slot in range(4):
            rows = slice(slot * BLOCK, (slot + 1) * BLOCK)
            lgf[slot, :, :LATENT] = nn(gkv[rows], w[...])
            lgf[slot, :, LATENT:] = jnp.where(mine, rope_grad[rows], 0.0)
            if slot == 1:
                lgs[0] = lgf[other].astype(BF16)
                lg_block.start()
        lgs[1] = lgf[2 + other].astype(BF16)
        lg_own.start()

    def combine():
        lg_block.wait_recv()
        lgs[2] = (lgf[core] + lgr[0].astype(F32)).astype(BF16)
        lg_back.start()

    def finish_plane(offset):
        step_three(pair_on(offset))
        step_four(pair_on(offset))

    lax.fori_loop(0, PAIRS // 2, attend, 0)
    step_two(pair_on(3))
    project()
    step_two(pair_on(4))
    lax.fori_loop(0, 2, query_grads, 0)
    combine()
    step_two(pair_on(5))
    lax.fori_loop(2, 4, query_grads, 0)
    step_two(pair_on(2))
    merge_near()
    step_two(pair_on(6))
    finish_plane(3)
    finish_plane(4)
    finish_plane(5)
    finish_plane(2)

    def finish_head(j, _):
        head = 2 * j + other
        remote(qg.at[j, sib_rows, pl.ds(0, DIM)], qn_out.at[:, columns(head)],
               g_send.at[0, j], g_recv.at[0, j], sibling).wait()
        remote(qr_in.at[j], qr_in.at[j], g_send.at[1, j], g_recv.at[1, j], sibling).wait()
        qr_out[:, columns(j)] = qg[j, own_rows, DIM:] + qr_in[j]
        remote(qd.at[j, sib_rows], qd.at[j, sib_rows], q_send.at[j], q_recv.at[j], sibling).wait_send()
        return 0

    lax.fori_loop(0, PAIRS, finish_head, 0)
    for n, device in enumerate((above, below)):
        remote(near_in.at[n], near_in.at[n], near_send.at[n], near_recv.at[n], device).wait_send()
    lg_own.wait_recv()
    lg_back.wait_recv()
    grads = lgf[2 + core] + lgr[1].astype(F32) + lgr[2].astype(F32)
    lat_out[...] = grads[:, :LATENT]
    tile = grads[:, LATENT:]
    rope_out[...] = jnp.transpose(tile + pltpu.roll(tile, ROPE, 1))[:ROPE]
    for copy in (rope_next, *lat_next, lat_sib, rope_sib, *lat_fwd, rope_fwd, lg_block, lg_own, lg_back):
        copy.wait_send()

    step_two(z)
    finish_plane(6)
    step_three(z)
    up_out[...] = zf[z]

    def add_plane(step, _):
        source = lax.rem(z + step, PAIRS)
        remote(zin.at[source], zin.at[source], z_send.at[source], z_recv.at[source], sibling).wait_recv()
        up_out[...] += zin[source].astype(F32)
        return 0

    lax.fori_loop(2, PAIRS - 1, add_plane, 0)

    def sums_ended(step, _):
        j = pair_on(step)
        for number, buffer in enumerate((in1, in2)):
            remote(buffer.at[j], buffer.at[j], rs_send.at[number, j], rs_recv.at[number, j], sibling).wait_send()
        return 0

    def plane_ended(step, _):
        j = pair_on(step)
        remote(zb.at[j], zb.at[j], z_send.at[j], z_recv.at[j], sibling).wait_send()
        return sums_ended(step, 0)

    lax.fori_loop(2, PAIRS - 1, plane_ended, 0)
    sums_ended(0, 0)


def fused(*arrays):
    hbm = pl.BlockSpec(memory_space=pltpu.HBM)
    dma = pltpu.SemaphoreType.DMA
    scratch = [
        pltpu.VMEM((512, LATENT), BF16),
        pltpu.VMEM((4, ROPE, BLOCK), BF16),
        pltpu.VMEM((512, DIM), BF16),
        pltpu.VMEM((1, 512), jnp.int32),
        pltpu.VMEM((512, 256), F32),
        pltpu.VMEM((PAIRS * 256, LATENT), BF16),
        pltpu.VMEM((PAIRS, 256, 3 * DIM), BF16),
        pltpu.VMEM((PAIRS, 256, 256), BF16),
        pltpu.VMEM((PAIRS, BLOCK, DIM), BF16),
        pltpu.VMEM((512, PAIRS * 256), BF16),
        pltpu.VMEM((512, DIM), F32),
        pltpu.VMEM((4, BLOCK, LATENT + DIM), F32),
        pltpu.VMEM((3, BLOCK, LATENT + DIM), BF16),
        pltpu.VMEM((3, BLOCK, LATENT + DIM), BF16),
        pltpu.VMEM((256, PAIRS * 256), BF16),
        pltpu.VMEM((PAIRS, 256, 256), F32),
        pltpu.VMEM((PAIRS, 256, 256), F32),
        pltpu.VMEM((PAIRS, 512, 256), BF16),
        pltpu.VMEM((PAIRS, 512, 256), BF16),
        pltpu.VMEM((PAIRS, 2, 4, 4, 16, 256), BF16),
        pltpu.VMEM((PAIRS, 2, 3, 4, 16, 256), BF16),
        pltpu.VMEM((PAIRS, 2, 4, 16, 256), F32),
        pltpu.VMEM((PAIRS, 2, 4, 16, 256), BF16),
        pltpu.VMEM((PAIRS, 2, 3, 16, 256), BF16),
        pltpu.VMEM((2, 2, 4, 4, 16, 256), BF16),
        pltpu.VMEM((PAIRS, 16, LATENT), F32),
        pltpu.VMEM((PAIRS, 16, LATENT), BF16),
        pltpu.VMEM((PAIRS, 16, LATENT), BF16),
        dma((4,)), dma((PAIRS,)), dma((PAIRS,)),
        dma((4 + 2 * CHUNKS,)), dma((4 + 2 * CHUNKS,)), dma((PAIRS,)), dma((PAIRS,)),
        dma((2, PAIRS)), dma((2, PAIRS)), dma((3,)), dma((3,)),
        dma((STEPS, PAIRS)), dma((STEPS, PAIRS)), dma((PAIRS,)), dma((PAIRS,)), dma((2,)), dma((2,)),
    ]
    return pl.pallas_call(
        kernel,
        out_shape=(
            jax.ShapeDtypeStruct((BLOCK, 2048), BF16),
            jax.ShapeDtypeStruct((BLOCK, 1024), BF16),
            jax.ShapeDtypeStruct((BLOCK, LATENT), F32),
            jax.ShapeDtypeStruct((ROPE, BLOCK), F32),
            jax.ShapeDtypeStruct((16, LATENT), F32),
        ),
        in_specs=[hbm] * 7,
        out_specs=(pl.BlockSpec(memory_space=pltpu.VMEM),) * 5,
        scratch_shapes=scratch,
        compiler_params=pltpu.CompilerParams(
            collective_id=0, has_side_effects=True, vmem_limit_bytes=VMEM_BYTES
        ),
        name="latent_attention_grads",
    )(*(pltpu.with_memory_space_constraint(a, pltpu.HBM) for a in arrays))


def write_kernel(count, *refs):
    sources, targets, sems = refs[:count], refs[count:2 * count], refs[2 * count]
    copies = [pltpu.make_async_copy(sources[n], targets[n], sems.at[n]) for n in range(count)]
    for copy in copies:
        copy.start()
    for copy in copies:
        copy.wait()


def write(values):
    count = len(values)
    return pl.pallas_call(
        functools.partial(write_kernel, count),
        out_shape=tuple(jax.ShapeDtypeStruct(value.shape, value.dtype) for value in values),
        in_specs=[pl.BlockSpec(memory_space=pltpu.VMEM)] * count,
        out_specs=(pl.BlockSpec(memory_space=pltpu.HBM),) * count,
        scratch_shapes=[pltpu.SemaphoreType.DMA((count,))],
        name="write_results",
    )(*(pltpu.with_memory_space_constraint(v, pltpu.VMEM) for v in values))


def body(q_nope, q_rope, dout, latent, rope_key, doc_ids, w_up):
    outs = write(fused(
        q_nope[0], q_rope[0], dout[0], latent[0], rope_key[0].T, doc_ids,
        w_up.reshape(2, PAIRS, 2, DIM, LATENT),
    ))
    return (outs[0][None], outs[1][None], outs[2][None], outs[3].T[None], outs[4])


def solution(mesh):
    return jax.shard_map(
        body,
        mesh=mesh,
        in_specs=(
            P("dp", "ctx", None),
            P("dp", "ctx", None),
            P("dp", "ctx", None),
            P("dp", "ctx", None),
            P("dp", "ctx", None),
            P("dp", None),
            P(),
        ),
        out_specs=(
            P("dp", "ctx", None),
            P("dp", "ctx", None),
            P("dp", "ctx", None),
            P("dp", "ctx", None),
            P(("ctx", "dp"), None),
        ),
        check_vma=False,
    )
```

```python
import functools

import jax
import jax.numpy as jnp
from jax import lax
from jax.experimental import pallas as pl
from jax.experimental.pallas import tpu as pltpu
from jax.sharding import PartitionSpec as P

LATENT = 512
ROPE = 64
DIM = 128
BLOCK = 128
PAIRS = 8
CHIPS = 16
CHUNKS = 4
CHUNK = BLOCK // CHUNKS
VMEM_BYTES = 40 * 1024 * 1024
STEPS = 2
SCALE = float(DIM + ROPE) ** -0.5
LOG2E = 1.4426950408889634
F32 = jnp.float32
BF16 = jnp.bfloat16


def nt(a, b):
    return lax.dot_general(a, b, (((1,), (1,)), ((), ())), preferred_element_type=F32)


def nn(a, b):
    return lax.dot_general(a, b, (((1,), (0,)), ((), ())), preferred_element_type=F32)


def tn(a, b):
    return lax.dot_general(a, b, (((0,), (0,)), ((), ())), preferred_element_type=F32)


def offsets(turn):
    late = turn // 2
    return 3 + turn, (1 + 6 * turn) * (1 - late) + (6 - 2 * turn) * late


def kernel(
    q_nope, q_rope, dout, latent, rope_key, docs, w_up,
    qn_out, qr_out, lat_out, rope_out, up_out,
    lat, ropes, rope_tile, doc_row, bias, w, qd, qg, qr_in, gkv, rope_grad, lgf, lgs, lgr,
    kv_own, scores_own, products_own, own_rows_of, grad_scores_kept, k_kept, part, in1, total, out2, in2, near_in, zf, zb, zin,
    local_sem, head_sem, w_sem,
    lat_send, lat_recv, q_send, q_recv, g_send, g_recv, lg_send, lg_recv,
    rs_send, rs_recv, z_send, z_recv, near_send, near_recv,
):
    ctx = lax.axis_index("ctx")
    dp = lax.axis_index("dp")
    core = lax.rem(ctx, 2)
    other = 1 - core
    chip = lax.div(ctx, 2)
    x_lo, z = lax.div(chip, PAIRS), lax.rem(chip, PAIRS)
    y, x_hi = lax.div(dp, 2), lax.rem(dp, 2)

    def at(ctx_index, dp_index):
        return {"ctx": ctx_index, "dp": dp_index}

    def place(xh, xl, yy, zz):
        return at((xl * PAIRS + zz) * 2 + core, yy * 2 + xh)

    sibling = at(chip * 2 + other, dp)
    after = at(lax.rem(chip + 1, CHIPS) * 2 + core, dp)
    before = at(lax.rem(chip + CHIPS - 1, CHIPS) * 2 + core, dp)
    x = x_hi * 2 + x_lo

    def x_on(step):
        to = lax.rem(x + step, 4)
        return place(lax.div(to, 2), lax.rem(to, 2), y, z)

    def y_on(step):
        return place(x_hi, x_lo, lax.rem(y + step, 4), z)

    above = place(x_hi, x_lo, y, lax.rem(z + 1, PAIRS))
    below = place(x_hi, x_lo, y, lax.rem(z + PAIRS - 1, PAIRS))
    first = ((x, x_on), (y, y_on))
    second = ((y, y_on), (x, x_on))

    own_rows = pl.ds(pl.multiple_of(core * BLOCK, BLOCK), BLOCK)
    sib_rows = pl.ds(pl.multiple_of(other * BLOCK, BLOCK), BLOCK)

    def lat_rows(slot):
        return pl.ds(pl.multiple_of(slot * BLOCK, BLOCK), BLOCK)

    def columns(index):
        return pl.ds(pl.multiple_of(index * DIM, DIM), DIM)

    def remote(src, dst, send, recv, device):
        return pltpu.make_async_remote_copy(
            src_ref=src, dst_ref=dst, send_sem=send, recv_sem=recv,
            device_id=device, device_id_type=pl.DeviceIdType.MESH,
        )

    barrier = pltpu.get_barrier_semaphore()

    def greet(device):
        pl.semaphore_signal(barrier, inc=1, device_id=device, device_id_type=pl.DeviceIdType.MESH)

    for device in (sibling, after, before):
        greet(device)
    for step in range(1, 4):
        greet(x_on(step))
        greet(y_on(step))
    for step in range(1, PAIRS):
        greet(place(x_hi, x_lo, y, lax.rem(z + step, PAIRS)))

    pltpu.make_async_copy(latent, lat.at[lat_rows(2 + core)], local_sem.at[0]).start()
    pltpu.make_async_copy(rope_key, ropes.at[2 + core], local_sem.at[1]).start()
    behind = lax.rem(chip + CHIPS - 1, CHIPS)
    doc_copies = (
        pltpu.make_async_copy(
            docs.at[:, pl.ds(pl.multiple_of(behind * 256, 256), 256)],
            doc_row.at[:, pl.ds(0, 256)], local_sem.at[2]),
        pltpu.make_async_copy(
            docs.at[:, pl.ds(pl.multiple_of(chip * 256, 256), 256)],
            doc_row.at[:, pl.ds(256, 256)], local_sem.at[3]),
    )
    for copy in doc_copies:
        copy.start()

    def load_head(j, _):
        head = 2 * j + core
        for half in range(2):
            pltpu.make_async_copy(
                w_up.at[half, j, core],
                w.at[pl.ds(pl.multiple_of(j * 256 + half * DIM, DIM), DIM)], w_sem.at[j]).start()
        pltpu.make_async_copy(
            q_nope.at[:, columns(head)], qd.at[j, own_rows, pl.ds(0, DIM)], head_sem.at[j]).start()
        pltpu.make_async_copy(
            q_rope.at[:, columns(j)], qd.at[j, own_rows, pl.ds(DIM, DIM)], head_sem.at[j]).start()
        pltpu.make_async_copy(
            dout.at[:, columns(head)], qd.at[j, own_rows, pl.ds(2 * DIM, DIM)], head_sem.at[j]).start()
        return 0

    lax.fori_loop(0, PAIRS, load_head, 0)

    pl.semaphore_wait(barrier, 8 + PAIRS)


    def lat_chunk(slot, chunk):
        return pl.ds(pl.multiple_of(slot * BLOCK + chunk * CHUNK, CHUNK), CHUNK)

    rope_next = remote(rope_key, ropes.at[core], lat_send.at[0], lat_recv.at[0], after)
    rope_sib = remote(rope_key, ropes.at[2 + core], lat_send.at[1], lat_recv.at[1], sibling)
    rope_fwd = remote(ropes.at[core], ropes.at[core], lat_send.at[2], lat_recv.at[2], sibling)
    lat_sib = remote(latent, lat.at[lat_rows(2 + core)], lat_send.at[3], lat_recv.at[3], sibling)
    lat_next = [
        remote(latent.at[pl.ds(n * CHUNK, CHUNK)], lat.at[lat_chunk(core, n)],
               lat_send.at[4 + n], lat_recv.at[4 + n], after)
        for n in range(CHUNKS)
    ]
    lat_fwd = [
        remote(lat.at[lat_chunk(core, n)], lat.at[lat_chunk(core, n)],
               lat_send.at[4 + CHUNKS + n], lat_recv.at[4 + CHUNKS + n], sibling)
        for n in range(CHUNKS)
    ]
    for copy in (rope_next, *lat_next, lat_sib, rope_sib):
        copy.start()

    def send_head(j, _):
        head = 2 * j + other
        remote(q_nope.at[:, columns(head)], qd.at[j, own_rows, pl.ds(0, DIM)],
               q_send.at[j], q_recv.at[j], sibling).start()
        remote(q_rope.at[:, columns(j)], qd.at[j, own_rows, pl.ds(DIM, DIM)],
               q_send.at[j], q_recv.at[j], sibling).start()
        remote(dout.at[:, columns(head)], qd.at[j, own_rows, pl.ds(2 * DIM, DIM)],
               q_send.at[j], q_recv.at[j], sibling).start()
        return 0

    lax.fori_loop(0, PAIRS, send_head, 0)

    for copy in doc_copies:
        copy.wait()
    row = doc_row[...].astype(F32)
    key_docs = jnp.transpose(jnp.broadcast_to(row, (DIM, 512)))
    key_docs = jnp.concatenate([key_docs, key_docs], axis=1)
    query_docs = jnp.broadcast_to(row[:, 256:], (512, 256))
    key_at = lax.broadcasted_iota(jnp.int32, (512, 256), 0)
    query_at = lax.broadcasted_iota(jnp.int32, (512, 256), 1)
    first_key = jnp.where(chip == 0, 256, 0)
    seen = (
        (key_at <= query_at + 256) & (key_at > query_at) & (key_at >= first_key)
        & (key_docs == query_docs)
    )
    bias[...] = jnp.where(seen, 0.0, -jnp.inf)
    rope_grad[...] = jnp.zeros_like(rope_grad)

    pltpu.make_async_copy(latent, lat.at[lat_rows(2 + core)], local_sem.at[0]).wait()
    pltpu.make_async_copy(rope_key, ropes.at[2 + core], local_sem.at[1]).wait()
    lat_sib.wait_recv()
    rope_sib.wait_recv()

    spread_row = lax.broadcasted_iota(jnp.int32, (ROPE, DIM), 0)
    spread_col = lax.broadcasted_iota(jnp.int32, (ROPE, DIM), 1)
    spread = jnp.where(spread_col == spread_row + core * ROPE, 1.0, 0.0).astype(BF16)

    def spread_rope(slot):
        rope_tile[slot * BLOCK:(slot + 1) * BLOCK] = tn(ropes[slot], spread).astype(BF16)

    spread_rope(2)
    spread_rope(3)

    def wait_weights(j, _):
        w_rows = pl.ds(pl.multiple_of(j * 256, 256), 256)
        pltpu.make_async_copy(w.at[w_rows], w.at[w_rows], w_sem.at[j]).wait()
        return 0

    lax.fori_loop(0, PAIRS, wait_weights, 0)
    kv_own[...] = nt(lat[256:], w[...]).astype(BF16)

    def own_keys(i, _):
        heads = (2 * i, 2 * i + 1)
        for j in heads:
            pltpu.make_async_copy(qd.at[j, own_rows], qd.at[j, own_rows], head_sem.at[j]).wait()
            remote(qd.at[j, sib_rows], qd.at[j, sib_rows], q_send.at[j], q_recv.at[j], sibling).wait_recv()
        kv = kv_own[:, pl.ds(pl.multiple_of(i * 512, 512), 512)]
        rope = rope_tile[256:]
        keys = [jnp.concatenate([kv[:, n * 256:n * 256 + DIM], rope], axis=1) for n in range(2)]
        scores = [nt(keys[n], qd[j, :, :256]) for n, j in enumerate(heads)]
        products = [nt(kv[:, n * 256 + DIM:(n + 1) * 256], qd[j, :, 256:]) for n, j in enumerate(heads)]
        for n, j in enumerate(heads):
            k_kept[j, 256:] = keys[n]
            score = scores[n] * (SCALE * LOG2E) + bias[256:]
            highest = jnp.max(score, axis=0, keepdims=True)
            weights = jnp.exp2(score - highest)
            scores_own[j] = weights
            products_own[j] = products[n]
            own_rows_of[j, 0:1] = highest
            own_rows_of[j, 1:2] = jnp.sum(weights, axis=0, keepdims=True)
            own_rows_of[j, 2:3] = jnp.sum(weights * products[n], axis=0, keepdims=True)
        return 0

    lax.fori_loop(0, PAIRS // 2, own_keys, 0)
    rope_next.wait_recv()
    rope_fwd.start()
    for arriving, onward in zip(lat_next, lat_fwd):
        arriving.wait_recv()
        onward.start()
    rope_fwd.wait_recv()
    spread_rope(0)
    spread_rope(1)
    for copy in lat_fwd:
        copy.wait_recv()

    def pair_on(offset):
        return lax.rem(z + offset, PAIRS)

    def send_part(j, half, index, step, on):
        remote(part.at[j, half, index], in1.at[j, half, step - 1],
               rs_send.at[0, j], rs_recv.at[0, j], on(step)).start()

    def send_first(j):
        for half, (index, on) in enumerate(first):
            for step in range(1, 4):
                send_part(j, half, lax.rem(index + step, 4), step, on)

    def attend(i, _):
        heads = [pair_on(offset) for offset in offsets(i)]
        kv = [nt(lat[:256], w[pl.ds(pl.multiple_of(j * 256, 256), 256)]).astype(BF16) for j in heads]
        rope = rope_tile[:256]
        keys = [jnp.concatenate([kv[n][:, :DIM], rope], axis=1) for n in range(2)]
        scores = [nt(keys[n], qd[j, :, :256]) for n, j in enumerate(heads)]
        products = [nt(kv[n][:, DIM:], qd[j, :, 256:]) for n, j in enumerate(heads)]
        probs_low, grad_scores = [], []
        for n, j in enumerate(heads):
            k_kept[j, :256] = keys[n]
            score = scores[n] * (SCALE * LOG2E) + bias[:256]
            own_highest = own_rows_of[j, 0:1]
            highest = jnp.maximum(jnp.max(score, axis=0, keepdims=True), own_highest)
            weights = jnp.exp2(score - highest)
            factor = jnp.exp2(own_highest - highest)
            inverse = 1.0 / (jnp.sum(weights, axis=0, keepdims=True) + own_rows_of[j, 1:2] * factor)
            probs = jnp.concatenate([weights * inverse, scores_own[j] * (factor * inverse)], axis=0)
            delta = (
                jnp.sum(weights * products[n], axis=0, keepdims=True) + own_rows_of[j, 2:3] * factor
            ) * inverse
            grad_probs = jnp.concatenate([products[n], products_own[j]], axis=0)
            probs_low.append(probs.astype(BF16))
            grad_scores.append((probs * ((grad_probs - delta) * SCALE)).astype(BF16))
        rope_sum = rope_grad[...]
        both = []
        for n, j in enumerate(heads):
            key_grad = nn(grad_scores[n], qd[j, :, :256])
            value_grad = nn(probs_low[n], qd[j, :, 256:])
            rope_sum = rope_sum + key_grad[:, DIM:]
            both.append(jnp.concatenate([key_grad[:, :DIM].astype(BF16), value_grad.astype(BF16)], axis=1))
        rope_grad[...] = rope_sum
        for n, j in enumerate(heads):
            gkv[:, pl.ds(pl.multiple_of(j * 256, 256), 256)] = both[n]
        ups = [tn(both[n], lat[...]).astype(BF16) for n in range(2)]
        for n, j in enumerate(heads):
            for to_x in range(4):
                for to_y in range(4):
                    start = to_x % 2 * DIM + to_y * 32 + to_x // 2 * 16
                    part[j, 0, to_x, to_y] = ups[n][start:start + 16, :256]
                    part[j, 1, to_y, to_x] = ups[n][start:start + 16, 256:]
        send_first(heads[0])
        pl.when(i == 0)(lambda: remote(
            part.at[heads[1]], near_in.at[0], near_send.at[0], near_recv.at[0], above).start())
        pl.when(i == 1)(lambda: remote(
            part.at[heads[1]], near_in.at[1], near_send.at[1], near_recv.at[1], below).start())
        pl.when(i == 2)(lambda: send_first(heads[1]))
        for n, j in enumerate(heads):
            grad_scores_kept[j] = grad_scores[n]
        return 0

    def merge_near():
        for n, device in enumerate((above, below)):
            remote(near_in.at[n], near_in.at[n], near_send.at[n], near_recv.at[n], device).wait_recv()

        for step in (2, 1, 3, 0):
            for half, (own, on) in enumerate(first):
                index = lax.rem(own + step, 4)
                part[z, half, index] = (
                    part[z, half, index].astype(F32)
                    + near_in[0, half, index].astype(F32) + near_in[1, half, index].astype(F32)
                ).astype(BF16)
                if step:
                    send_part(z, half, index, step, on)

    def query_grads(i, _):
        heads = (2 * i, 2 * i + 1)
        grads = [tn(grad_scores_kept[j], k_kept[j]).astype(BF16) for j in heads]
        for n, j in enumerate(heads):
            qg[j] = grads[n]
            head = 2 * j + core
            remote(qg.at[j, sib_rows, pl.ds(0, DIM)], qn_out.at[:, columns(head)],
                   g_send.at[0, j], g_recv.at[0, j], sibling).start()
            remote(qg.at[j, sib_rows, pl.ds(DIM, DIM)], qr_in.at[j],
                   g_send.at[1, j], g_recv.at[1, j], sibling).start()
            qn_out[:, columns(head)] = qg[j, own_rows, :DIM]
        return 0

    def arrived(buffer, step, j):
        remote(buffer.at[j], buffer.at[j], rs_send.at[step, j], rs_recv.at[step, j], sibling).wait_recv()

    def step_two(j):
        arrived(in1, 0, j)
        for half, (index, on) in enumerate(second):
            own, _ = first[half]
            summed = part[j, half, own].astype(F32)
            for step in range(3):
                summed = summed + in1[j, half, step].astype(F32)
            total[j, half] = summed
            out2[j, half] = summed.astype(BF16)
            for step in range(1, 4):
                remote(out2.at[j, half, lax.rem(index + step, 4)], in2.at[j, half, step - 1],
                       rs_send.at[1, j], rs_recv.at[1, j], on(step)).start()

    def step_three(j):
        arrived(in2, 1, j)
        for half, (own, _) in enumerate(second):
            summed = total[j, half, own]
            for step in range(3):
                summed = summed + in2[j, half, step].astype(F32)
            zf[j, :, half * 256:(half + 1) * 256] = summed
            zb[j, :, half * 256:(half + 1) * 256] = summed.astype(BF16)

    def step_four(j):
        remote(zb.at[j], zin.at[z], z_send.at[j], z_recv.at[z], place(x_hi, x_lo, y, j)).start()

    lg_block = remote(lgs.at[0], lgr.at[0], lg_send.at[0], lg_recv.at[0], sibling)
    lg_own = remote(lgs.at[1], lgr.at[1], lg_send.at[1], lg_recv.at[1], sibling)
    lg_back = remote(lgs.at[2], lgr.at[2], lg_send.at[2], lg_recv.at[2], before)

    def project():
        lane = lax.broadcasted_iota(jnp.int32, (BLOCK, DIM), 1)
        mine = (lane >= core * ROPE) & (lane < (core + 1) * ROPE)
        for slot in range(4):
            rows = slice(slot * BLOCK, (slot + 1) * BLOCK)
            lgf[slot, :, :LATENT] = nn(gkv[rows], w[...])
            lgf[slot, :, LATENT:] = jnp.where(mine, rope_grad[rows], 0.0)
            if slot == 1:
                lgs[0] = lgf[other].astype(BF16)
                lg_block.start()
        lgs[1] = lgf[2 + other].astype(BF16)
        lg_own.start()

    def combine():
        lg_block.wait_recv()
        lgs[2] = (lgf[core] + lgr[0].astype(F32)).astype(BF16)
        lg_back.start()

    def finish_plane(offset):
        step_three(pair_on(offset))
        step_four(pair_on(offset))

    lax.fori_loop(0, PAIRS // 2, attend, 0)
    step_two(pair_on(3))
    project()
    step_two(pair_on(4))
    lax.fori_loop(0, 2, query_grads, 0)
    combine()
    step_two(pair_on(5))
    lax.fori_loop(2, 4, query_grads, 0)
    step_two(pair_on(2))
    merge_near()
    step_two(pair_on(6))
    finish_plane(3)
    finish_plane(4)
    finish_plane(5)
    finish_plane(2)

    step_two(z)
    finish_plane(6)

    def finish_head(j, _):
        head = 2 * j + other
        remote(qg.at[j, sib_rows, pl.ds(0, DIM)], qn_out.at[:, columns(head)],
               g_send.at[0, j], g_recv.at[0, j], sibling).wait()
        remote(qr_in.at[j], qr_in.at[j], g_send.at[1, j], g_recv.at[1, j], sibling).wait()
        qr_out[:, columns(j)] = qg[j, own_rows, DIM:] + qr_in[j]
        remote(qd.at[j, sib_rows], qd.at[j, sib_rows], q_send.at[j], q_recv.at[j], sibling).wait_send()
        return 0

    lax.fori_loop(0, PAIRS, finish_head, 0)
    for n, device in enumerate((above, below)):
        remote(near_in.at[n], near_in.at[n], near_send.at[n], near_recv.at[n], device).wait_send()
    lg_own.wait_recv()
    lg_back.wait_recv()
    grads = lgf[2 + core] + lgr[1].astype(F32) + lgr[2].astype(F32)
    lat_out[...] = grads[:, :LATENT]
    tile = grads[:, LATENT:]
    rope_out[...] = jnp.transpose(tile + pltpu.roll(tile, ROPE, 1))[:ROPE]
    for copy in (rope_next, *lat_next, lat_sib, rope_sib, *lat_fwd, rope_fwd, lg_block, lg_own, lg_back):
        copy.wait_send()

    step_three(z)
    up_out[...] = zf[z]

    def add_plane(step, _):
        source = lax.rem(z + step, PAIRS)
        remote(zin.at[source], zin.at[source], z_send.at[source], z_recv.at[source], sibling).wait_recv()
        up_out[...] += zin[source].astype(F32)
        return 0

    lax.fori_loop(2, PAIRS - 1, add_plane, 0)

    def sums_ended(step, _):
        j = pair_on(step)
        for number, buffer in enumerate((in1, in2)):
            remote(buffer.at[j], buffer.at[j], rs_send.at[number, j], rs_recv.at[number, j], sibling).wait_send()
        return 0

    def plane_ended(step, _):
        j = pair_on(step)
        remote(zb.at[j], zb.at[j], z_send.at[j], z_recv.at[j], sibling).wait_send()
        return sums_ended(step, 0)

    lax.fori_loop(2, PAIRS - 1, plane_ended, 0)
    sums_ended(0, 0)


def fused(*arrays):
    hbm = pl.BlockSpec(memory_space=pltpu.HBM)
    dma = pltpu.SemaphoreType.DMA
    scratch = [
        pltpu.VMEM((512, LATENT), BF16),
        pltpu.VMEM((4, ROPE, BLOCK), BF16),
        pltpu.VMEM((512, DIM), BF16),
        pltpu.VMEM((1, 512), jnp.int32),
        pltpu.VMEM((512, 256), F32),
        pltpu.VMEM((PAIRS * 256, LATENT), BF16),
        pltpu.VMEM((PAIRS, 256, 3 * DIM), BF16),
        pltpu.VMEM((PAIRS, 256, 256), BF16),
        pltpu.VMEM((PAIRS, BLOCK, DIM), BF16),
        pltpu.VMEM((512, PAIRS * 256), BF16),
        pltpu.VMEM((512, DIM), F32),
        pltpu.VMEM((4, BLOCK, LATENT + DIM), F32),
        pltpu.VMEM((3, BLOCK, LATENT + DIM), BF16),
        pltpu.VMEM((3, BLOCK, LATENT + DIM), BF16),
        pltpu.VMEM((256, PAIRS * 256), BF16),
        pltpu.VMEM((PAIRS, 256, 256), F32),
        pltpu.VMEM((PAIRS, 256, 256), F32),
        pltpu.VMEM((PAIRS, 8, 256), F32),
        pltpu.VMEM((PAIRS, 512, 256), BF16),
        pltpu.VMEM((PAIRS, 512, 256), BF16),
        pltpu.VMEM((PAIRS, 2, 4, 4, 16, 256), BF16),
        pltpu.VMEM((PAIRS, 2, 3, 4, 16, 256), BF16),
        pltpu.VMEM((PAIRS, 2, 4, 16, 256), F32),
        pltpu.VMEM((PAIRS, 2, 4, 16, 256), BF16),
        pltpu.VMEM((PAIRS, 2, 3, 16, 256), BF16),
        pltpu.VMEM((2, 2, 4, 4, 16, 256), BF16),
        pltpu.VMEM((PAIRS, 16, LATENT), F32),
        pltpu.VMEM((PAIRS, 16, LATENT), BF16),
        pltpu.VMEM((PAIRS, 16, LATENT), BF16),
        dma((4,)), dma((PAIRS,)), dma((PAIRS,)),
        dma((4 + 2 * CHUNKS,)), dma((4 + 2 * CHUNKS,)), dma((PAIRS,)), dma((PAIRS,)),
        dma((2, PAIRS)), dma((2, PAIRS)), dma((3,)), dma((3,)),
        dma((STEPS, PAIRS)), dma((STEPS, PAIRS)), dma((PAIRS,)), dma((PAIRS,)), dma((2,)), dma((2,)),
    ]
    return pl.pallas_call(
        kernel,
        out_shape=(
            jax.ShapeDtypeStruct((BLOCK, 2048), BF16),
            jax.ShapeDtypeStruct((BLOCK, 1024), BF16),
            jax.ShapeDtypeStruct((BLOCK, LATENT), F32),
            jax.ShapeDtypeStruct((ROPE, BLOCK), F32),
            jax.ShapeDtypeStruct((16, LATENT), F32),
        ),
        in_specs=[hbm] * 7,
        out_specs=(pl.BlockSpec(memory_space=pltpu.VMEM),) * 5,
        scratch_shapes=scratch,
        compiler_params=pltpu.CompilerParams(
            collective_id=0, has_side_effects=True, vmem_limit_bytes=VMEM_BYTES
        ),
        name="latent_attention_grads",
    )(*(pltpu.with_memory_space_constraint(a, pltpu.HBM) for a in arrays))


def write_kernel(count, *refs):
    sources, targets, sems = refs[:count], refs[count:2 * count], refs[2 * count]
    copies = [pltpu.make_async_copy(sources[n], targets[n], sems.at[n]) for n in range(count)]
    for copy in copies:
        copy.start()
    for copy in copies:
        copy.wait()


def write(values):
    count = len(values)
    return pl.pallas_call(
        functools.partial(write_kernel, count),
        out_shape=tuple(jax.ShapeDtypeStruct(value.shape, value.dtype) for value in values),
        in_specs=[pl.BlockSpec(memory_space=pltpu.VMEM)] * count,
        out_specs=(pl.BlockSpec(memory_space=pltpu.HBM),) * count,
        scratch_shapes=[pltpu.SemaphoreType.DMA((count,))],
        name="write_results",
    )(*(pltpu.with_memory_space_constraint(v, pltpu.VMEM) for v in values))


def body(q_nope, q_rope, dout, latent, rope_key, doc_ids, w_up):
    outs = write(fused(
        q_nope[0], q_rope[0], dout[0], latent[0], rope_key[0].T, doc_ids,
        w_up.reshape(2, PAIRS, 2, DIM, LATENT),
    ))
    return (outs[0][None], outs[1][None], outs[2][None], outs[3].T[None], outs[4])


def solution(mesh):
    return jax.shard_map(
        body,
        mesh=mesh,
        in_specs=(
            P("dp", "ctx", None),
            P("dp", "ctx", None),
            P("dp", "ctx", None),
            P("dp", "ctx", None),
            P("dp", "ctx", None),
            P("dp", None),
            P(),
        ),
        out_specs=(
            P("dp", "ctx", None),
            P("dp", "ctx", None),
            P("dp", "ctx", None),
            P("dp", "ctx", None),
            P(("ctx", "dp"), None),
        ),
        check_vma=False,
    )
```

```python
import functools

import jax
import jax.numpy as jnp
from jax import lax
from jax.experimental import pallas as pl
from jax.experimental.pallas import tpu as pltpu
from jax.sharding import PartitionSpec as P

LATENT = 512
ROPE = 64
DIM = 128
BLOCK = 128
PAIRS = 8
CHIPS = 16
CHUNKS = 4
CHUNK = BLOCK // CHUNKS
VMEM_BYTES = 40 * 1024 * 1024
STEPS = 2
SCALE = float(DIM + ROPE) ** -0.5
LOG2E = 1.4426950408889634
F32 = jnp.float32
BF16 = jnp.bfloat16


def nt(a, b):
    return lax.dot_general(a, b, (((1,), (1,)), ((), ())), preferred_element_type=F32)


def nn(a, b):
    return lax.dot_general(a, b, (((1,), (0,)), ((), ())), preferred_element_type=F32)


def tn(a, b):
    return lax.dot_general(a, b, (((0,), (0,)), ((), ())), preferred_element_type=F32)


def offsets(turn):
    late = turn // 2
    return 3 + turn, (1 + 6 * turn) * (1 - late) + (6 - 2 * turn) * late


def kernel(
    q_nope, q_rope, dout, latent, rope_key, docs, w_up,
    qn_out, qr_out, lat_out, rope_out, up_out,
    lat, ropes, rope_tile, doc_row, bias, w, qd, qg, qr_in, gkv, rope_grad, lgf, lgs, lgr,
    kv_own, kv_held, scores_own, products_own, own_rows_of, grad_scores_kept, k_kept, part, in1, total, out2, in2, near_in, zf, zb, zin,
    local_sem, head_sem, w_sem,
    lat_send, lat_recv, q_send, q_recv, g_send, g_recv, lg_send, lg_recv,
    rs_send, rs_recv, z_send, z_recv, near_send, near_recv,
):
    ctx = lax.axis_index("ctx")
    dp = lax.axis_index("dp")
    core = lax.rem(ctx, 2)
    other = 1 - core
    chip = lax.div(ctx, 2)
    x_lo, z = lax.div(chip, PAIRS), lax.rem(chip, PAIRS)
    y, x_hi = lax.div(dp, 2), lax.rem(dp, 2)

    def at(ctx_index, dp_index):
        return {"ctx": ctx_index, "dp": dp_index}

    def place(xh, xl, yy, zz):
        return at((xl * PAIRS + zz) * 2 + core, yy * 2 + xh)

    sibling = at(chip * 2 + other, dp)
    after = at(lax.rem(chip + 1, CHIPS) * 2 + core, dp)
    before = at(lax.rem(chip + CHIPS - 1, CHIPS) * 2 + core, dp)
    x = x_hi * 2 + x_lo

    def x_on(step):
        to = lax.rem(x + step, 4)
        return place(lax.div(to, 2), lax.rem(to, 2), y, z)

    def y_on(step):
        return place(x_hi, x_lo, lax.rem(y + step, 4), z)

    above = place(x_hi, x_lo, y, lax.rem(z + 1, PAIRS))
    below = place(x_hi, x_lo, y, lax.rem(z + PAIRS - 1, PAIRS))
    first = ((x, x_on), (y, y_on))
    second = ((y, y_on), (x, x_on))

    own_rows = pl.ds(pl.multiple_of(core * BLOCK, BLOCK), BLOCK)
    sib_rows = pl.ds(pl.multiple_of(other * BLOCK, BLOCK), BLOCK)

    def lat_rows(slot):
        return pl.ds(pl.multiple_of(slot * BLOCK, BLOCK), BLOCK)

    def columns(index):
        return pl.ds(pl.multiple_of(index * DIM, DIM), DIM)

    def remote(src, dst, send, recv, device):
        return pltpu.make_async_remote_copy(
            src_ref=src, dst_ref=dst, send_sem=send, recv_sem=recv,
            device_id=device, device_id_type=pl.DeviceIdType.MESH,
        )

    barrier = pltpu.get_barrier_semaphore()

    def greet(device):
        pl.semaphore_signal(barrier, inc=1, device_id=device, device_id_type=pl.DeviceIdType.MESH)

    for device in (sibling, after, before):
        greet(device)
    for step in range(1, 4):
        greet(x_on(step))
        greet(y_on(step))
    for step in range(1, PAIRS):
        greet(place(x_hi, x_lo, y, lax.rem(z + step, PAIRS)))

    pltpu.make_async_copy(latent, lat.at[lat_rows(2 + core)], local_sem.at[0]).start()
    pltpu.make_async_copy(rope_key, ropes.at[2 + core], local_sem.at[1]).start()
    behind = lax.rem(chip + CHIPS - 1, CHIPS)
    doc_copies = (
        pltpu.make_async_copy(
            docs.at[:, pl.ds(pl.multiple_of(behind * 256, 256), 256)],
            doc_row.at[:, pl.ds(0, 256)], local_sem.at[2]),
        pltpu.make_async_copy(
            docs.at[:, pl.ds(pl.multiple_of(chip * 256, 256), 256)],
            doc_row.at[:, pl.ds(256, 256)], local_sem.at[3]),
    )
    for copy in doc_copies:
        copy.start()

    def load_head(j, _):
        head = 2 * j + core
        for half in range(2):
            pltpu.make_async_copy(
                w_up.at[half, j, core],
                w.at[pl.ds(pl.multiple_of(j * 256 + half * DIM, DIM), DIM)], w_sem.at[j]).start()
        pltpu.make_async_copy(
            q_nope.at[:, columns(head)], qd.at[j, own_rows, pl.ds(0, DIM)], head_sem.at[j]).start()
        pltpu.make_async_copy(
            q_rope.at[:, columns(j)], qd.at[j, own_rows, pl.ds(DIM, DIM)], head_sem.at[j]).start()
        pltpu.make_async_copy(
            dout.at[:, columns(head)], qd.at[j, own_rows, pl.ds(2 * DIM, DIM)], head_sem.at[j]).start()
        return 0

    lax.fori_loop(0, PAIRS, load_head, 0)

    pl.semaphore_wait(barrier, 8 + PAIRS)


    def lat_chunk(slot, chunk):
        return pl.ds(pl.multiple_of(slot * BLOCK + chunk * CHUNK, CHUNK), CHUNK)

    rope_next = remote(rope_key, ropes.at[core], lat_send.at[0], lat_recv.at[0], after)
    rope_sib = remote(rope_key, ropes.at[2 + core], lat_send.at[1], lat_recv.at[1], sibling)
    rope_fwd = remote(ropes.at[core], ropes.at[core], lat_send.at[2], lat_recv.at[2], sibling)
    lat_sib = remote(latent, lat.at[lat_rows(2 + core)], lat_send.at[3], lat_recv.at[3], sibling)
    lat_next = [
        remote(latent.at[pl.ds(n * CHUNK, CHUNK)], lat.at[lat_chunk(core, n)],
               lat_send.at[4 + n], lat_recv.at[4 + n], after)
        for n in range(CHUNKS)
    ]
    lat_fwd = [
        remote(lat.at[lat_chunk(core, n)], lat.at[lat_chunk(core, n)],
               lat_send.at[4 + CHUNKS + n], lat_recv.at[4 + CHUNKS + n], sibling)
        for n in range(CHUNKS)
    ]
    for copy in (rope_next, *lat_next, lat_sib, rope_sib):
        copy.start()

    def send_head(j, _):
        head = 2 * j + other
        remote(q_nope.at[:, columns(head)], qd.at[j, own_rows, pl.ds(0, DIM)],
               q_send.at[j], q_recv.at[j], sibling).start()
        remote(q_rope.at[:, columns(j)], qd.at[j, own_rows, pl.ds(DIM, DIM)],
               q_send.at[j], q_recv.at[j], sibling).start()
        remote(dout.at[:, columns(head)], qd.at[j, own_rows, pl.ds(2 * DIM, DIM)],
               q_send.at[j], q_recv.at[j], sibling).start()
        return 0

    lax.fori_loop(0, PAIRS, send_head, 0)

    for copy in doc_copies:
        copy.wait()
    row = doc_row[...].astype(F32)
    key_docs = jnp.transpose(jnp.broadcast_to(row, (DIM, 512)))
    key_docs = jnp.concatenate([key_docs, key_docs], axis=1)
    query_docs = jnp.broadcast_to(row[:, 256:], (512, 256))
    key_at = lax.broadcasted_iota(jnp.int32, (512, 256), 0)
    query_at = lax.broadcasted_iota(jnp.int32, (512, 256), 1)
    first_key = jnp.where(chip == 0, 256, 0)
    seen = (
        (key_at <= query_at + 256) & (key_at > query_at) & (key_at >= first_key)
        & (key_docs == query_docs)
    )
    bias[...] = jnp.where(seen, 0.0, -jnp.inf)
    rope_grad[...] = jnp.zeros_like(rope_grad)

    pltpu.make_async_copy(latent, lat.at[lat_rows(2 + core)], local_sem.at[0]).wait()
    pltpu.make_async_copy(rope_key, ropes.at[2 + core], local_sem.at[1]).wait()
    lat_sib.wait_recv()
    rope_sib.wait_recv()

    spread_row = lax.broadcasted_iota(jnp.int32, (ROPE, DIM), 0)
    spread_col = lax.broadcasted_iota(jnp.int32, (ROPE, DIM), 1)
    spread = jnp.where(spread_col == spread_row + core * ROPE, 1.0, 0.0).astype(BF16)

    def spread_rope(slot):
        rope_tile[slot * BLOCK:(slot + 1) * BLOCK] = tn(ropes[slot], spread).astype(BF16)

    spread_rope(2)
    spread_rope(3)

    def wait_weights(j, _):
        w_rows = pl.ds(pl.multiple_of(j * 256, 256), 256)
        pltpu.make_async_copy(w.at[w_rows], w.at[w_rows], w_sem.at[j]).wait()
        return 0

    lax.fori_loop(0, PAIRS, wait_weights, 0)
    kv_own[...] = nt(lat[256:], w[...]).astype(BF16)

    def own_keys(i, _):
        heads = (2 * i, 2 * i + 1)
        for j in heads:
            pltpu.make_async_copy(qd.at[j, own_rows], qd.at[j, own_rows], head_sem.at[j]).wait()
            remote(qd.at[j, sib_rows], qd.at[j, sib_rows], q_send.at[j], q_recv.at[j], sibling).wait_recv()
        kv = kv_own[:, pl.ds(pl.multiple_of(i * 512, 512), 512)]
        rope = rope_tile[256:]
        keys = [jnp.concatenate([kv[:, n * 256:n * 256 + DIM], rope], axis=1) for n in range(2)]
        scores = [nt(keys[n], qd[j, :, :256]) for n, j in enumerate(heads)]
        products = [nt(kv[:, n * 256 + DIM:(n + 1) * 256], qd[j, :, 256:]) for n, j in enumerate(heads)]
        for n, j in enumerate(heads):
            k_kept[j, 256:] = keys[n]
            score = scores[n] * (SCALE * LOG2E) + bias[256:]
            highest = jnp.max(score, axis=0, keepdims=True)
            weights = jnp.exp2(score - highest)
            scores_own[j] = weights
            products_own[j] = products[n]
            own_rows_of[j, 0:1] = highest
            own_rows_of[j, 1:2] = jnp.sum(weights, axis=0, keepdims=True)
            own_rows_of[j, 2:3] = jnp.sum(weights * products[n], axis=0, keepdims=True)
        return 0

    lax.fori_loop(0, PAIRS // 2, own_keys, 0)
    rope_next.wait_recv()
    rope_fwd.start()
    for arriving, onward in zip(lat_next, lat_fwd):
        arriving.wait_recv()
        onward.start()
    rope_fwd.wait_recv()
    spread_rope(0)
    spread_rope(1)
    for copy in lat_fwd:
        copy.wait_recv()

    def pair_on(offset):
        return lax.rem(z + offset, PAIRS)

    def send_part(j, half, index, step, on):
        remote(part.at[j, half, index], in1.at[j, half, step - 1],
               rs_send.at[0, j], rs_recv.at[0, j], on(step)).start()

    def send_first(j):
        for half, (index, on) in enumerate(first):
            for step in range(1, 4):
                send_part(j, half, lax.rem(index + step, 4), step, on)

    def expand(turn):
        for n, offset in enumerate(offsets(turn)):
            rows = pl.ds(pl.multiple_of(pair_on(offset) * 256, 256), 256)
            kv_held[n] = nt(lat[:256], w[rows]).astype(BF16)

    def attend(i, _):
        heads = [pair_on(offset) for offset in offsets(i)]
        kv = [kv_held[n] for n in range(2)]
        rope = rope_tile[:256]
        keys = [jnp.concatenate([kv[n][:, :DIM], rope], axis=1) for n in range(2)]
        scores = [nt(keys[n], qd[j, :, :256]) for n, j in enumerate(heads)]
        products = [nt(kv[n][:, DIM:], qd[j, :, 256:]) for n, j in enumerate(heads)]
        expand(lax.rem(i + 1, PAIRS // 2))
        probs_low, grad_scores = [], []
        for n, j in enumerate(heads):
            k_kept[j, :256] = keys[n]
            score = scores[n] * (SCALE * LOG2E) + bias[:256]
            own_highest = own_rows_of[j, 0:1]
            highest = jnp.maximum(jnp.max(score, axis=0, keepdims=True), own_highest)
            weights = jnp.exp2(score - highest)
            factor = jnp.exp2(own_highest - highest)
            inverse = 1.0 / (jnp.sum(weights, axis=0, keepdims=True) + own_rows_of[j, 1:2] * factor)
            probs = jnp.concatenate([weights * inverse, scores_own[j] * (factor * inverse)], axis=0)
            delta = (
                jnp.sum(weights * products[n], axis=0, keepdims=True) + own_rows_of[j, 2:3] * factor
            ) * inverse
            grad_probs = jnp.concatenate([products[n], products_own[j]], axis=0)
            probs_low.append(probs.astype(BF16))
            grad_scores.append((probs * ((grad_probs - delta) * SCALE)).astype(BF16))
        rope_sum = rope_grad[...]
        both = []
        for n, j in enumerate(heads):
            key_grad = nn(grad_scores[n], qd[j, :, :256])
            value_grad = nn(probs_low[n], qd[j, :, 256:])
            rope_sum = rope_sum + key_grad[:, DIM:]
            both.append(jnp.concatenate([key_grad[:, :DIM].astype(BF16), value_grad.astype(BF16)], axis=1))
        rope_grad[...] = rope_sum
        for n, j in enumerate(heads):
            gkv[:, pl.ds(pl.multiple_of(j * 256, 256), 256)] = both[n]
        ups = [tn(both[n], lat[...]).astype(BF16) for n in range(2)]
        for n, j in enumerate(heads):
            for to_x in range(4):
                for to_y in range(4):
                    start = to_x % 2 * DIM + to_y * 32 + to_x // 2 * 16
                    part[j, 0, to_x, to_y] = ups[n][start:start + 16, :256]
                    part[j, 1, to_y, to_x] = ups[n][start:start + 16, 256:]
        send_first(heads[0])
        pl.when(i == 0)(lambda: remote(
            part.at[heads[1]], near_in.at[0], near_send.at[0], near_recv.at[0], above).start())
        pl.when(i == 1)(lambda: remote(
            part.at[heads[1]], near_in.at[1], near_send.at[1], near_recv.at[1], below).start())
        pl.when(i == 2)(lambda: send_first(heads[1]))
        for n, j in enumerate(heads):
            grad_scores_kept[j] = grad_scores[n]
        return 0

    def merge_near():
        for n, device in enumerate((above, below)):
            remote(near_in.at[n], near_in.at[n], near_send.at[n], near_recv.at[n], device).wait_recv()

        for step in (2, 1, 3, 0):
            for half, (own, on) in enumerate(first):
                index = lax.rem(own + step, 4)
                part[z, half, index] = (
                    part[z, half, index].astype(F32)
                    + near_in[0, half, index].astype(F32) + near_in[1, half, index].astype(F32)
                ).astype(BF16)
                if step:
                    send_part(z, half, index, step, on)

    def query_grads(i, _):
        heads = (2 * i, 2 * i + 1)
        grads = [tn(grad_scores_kept[j], k_kept[j]).astype(BF16) for j in heads]
        for n, j in enumerate(heads):
            qg[j] = grads[n]
            head = 2 * j + core
            remote(qg.at[j, sib_rows, pl.ds(0, DIM)], qn_out.at[:, columns(head)],
                   g_send.at[0, j], g_recv.at[0, j], sibling).start()
            remote(qg.at[j, sib_rows, pl.ds(DIM, DIM)], qr_in.at[j],
                   g_send.at[1, j], g_recv.at[1, j], sibling).start()
            qn_out[:, columns(head)] = qg[j, own_rows, :DIM]
        return 0

    def arrived(buffer, step, j):
        remote(buffer.at[j], buffer.at[j], rs_send.at[step, j], rs_recv.at[step, j], sibling).wait_recv()

    def step_two(j):
        arrived(in1, 0, j)
        for half, (index, on) in enumerate(second):
            own, _ = first[half]
            summed = part[j, half, own].astype(F32)
            for step in range(3):
                summed = summed + in1[j, half, step].astype(F32)
            total[j, half] = summed
            out2[j, half] = summed.astype(BF16)
            for step in range(1, 4):
                remote(out2.at[j, half, lax.rem(index + step, 4)], in2.at[j, half, step - 1],
                       rs_send.at[1, j], rs_recv.at[1, j], on(step)).start()

    def step_three(j):
        arrived(in2, 1, j)
        for half, (own, _) in enumerate(second):
            summed = total[j, half, own]
            for step in range(3):
                summed = summed + in2[j, half, step].astype(F32)
            zf[j, :, half * 256:(half + 1) * 256] = summed
            zb[j, :, half * 256:(half + 1) * 256] = summed.astype(BF16)

    def step_four(j):
        remote(zb.at[j], zin.at[z], z_send.at[j], z_recv.at[z], place(x_hi, x_lo, y, j)).start()

    lg_block = remote(lgs.at[0], lgr.at[0], lg_send.at[0], lg_recv.at[0], sibling)
    lg_own = remote(lgs.at[1], lgr.at[1], lg_send.at[1], lg_recv.at[1], sibling)
    lg_back = remote(lgs.at[2], lgr.at[2], lg_send.at[2], lg_recv.at[2], before)

    def project():
        lane = lax.broadcasted_iota(jnp.int32, (BLOCK, DIM), 1)
        mine = (lane >= core * ROPE) & (lane < (core + 1) * ROPE)
        for slot in range(4):
            rows = slice(slot * BLOCK, (slot + 1) * BLOCK)
            lgf[slot, :, :LATENT] = nn(gkv[rows], w[...])
            lgf[slot, :, LATENT:] = jnp.where(mine, rope_grad[rows], 0.0)
            if slot == 1:
                lgs[0] = lgf[other].astype(BF16)
                lg_block.start()
        lgs[1] = lgf[2 + other].astype(BF16)
        lg_own.start()

    def combine():
        lg_block.wait_recv()
        lgs[2] = (lgf[core] + lgr[0].astype(F32)).astype(BF16)
        lg_back.start()

    def finish_plane(offset):
        step_three(pair_on(offset))
        step_four(pair_on(offset))

    expand(0)
    lax.fori_loop(0, PAIRS // 2, attend, 0)
    step_two(pair_on(3))
    project()
    step_two(pair_on(4))
    lax.fori_loop(0, 2, query_grads, 0)
    combine()
    step_two(pair_on(5))
    lax.fori_loop(2, 4, query_grads, 0)
    step_two(pair_on(2))
    merge_near()
    step_two(pair_on(6))
    finish_plane(3)
    finish_plane(4)
    finish_plane(5)
    finish_plane(2)

    step_two(z)
    finish_plane(6)

    def finish_head(j, _):
        head = 2 * j + other
        remote(qg.at[j, sib_rows, pl.ds(0, DIM)], qn_out.at[:, columns(head)],
               g_send.at[0, j], g_recv.at[0, j], sibling).wait()
        remote(qr_in.at[j], qr_in.at[j], g_send.at[1, j], g_recv.at[1, j], sibling).wait()
        qr_out[:, columns(j)] = qg[j, own_rows, DIM:] + qr_in[j]
        remote(qd.at[j, sib_rows], qd.at[j, sib_rows], q_send.at[j], q_recv.at[j], sibling).wait_send()
        return 0

    lax.fori_loop(0, PAIRS, finish_head, 0)
    for n, device in enumerate((above, below)):
        remote(near_in.at[n], near_in.at[n], near_send.at[n], near_recv.at[n], device).wait_send()
    lg_own.wait_recv()
    lg_back.wait_recv()
    grads = lgf[2 + core] + lgr[1].astype(F32) + lgr[2].astype(F32)
    lat_out[...] = grads[:, :LATENT]
    tile = grads[:, LATENT:]
    rope_out[...] = jnp.transpose(tile + pltpu.roll(tile, ROPE, 1))[:ROPE]
    for copy in (rope_next, *lat_next, lat_sib, rope_sib, *lat_fwd, rope_fwd, lg_block, lg_own, lg_back):
        copy.wait_send()

    step_three(z)
    up_out[...] = zf[z]

    def add_plane(step, _):
        source = lax.rem(z + step, PAIRS)
        remote(zin.at[source], zin.at[source], z_send.at[source], z_recv.at[source], sibling).wait_recv()
        up_out[...] += zin[source].astype(F32)
        return 0

    lax.fori_loop(2, PAIRS - 1, add_plane, 0)

    def sums_ended(step, _):
        j = pair_on(step)
        for number, buffer in enumerate((in1, in2)):
            remote(buffer.at[j], buffer.at[j], rs_send.at[number, j], rs_recv.at[number, j], sibling).wait_send()
        return 0

    def plane_ended(step, _):
        j = pair_on(step)
        remote(zb.at[j], zb.at[j], z_send.at[j], z_recv.at[j], sibling).wait_send()
        return sums_ended(step, 0)

    lax.fori_loop(2, PAIRS - 1, plane_ended, 0)
    sums_ended(0, 0)


def fused(*arrays):
    hbm = pl.BlockSpec(memory_space=pltpu.HBM)
    dma = pltpu.SemaphoreType.DMA
    scratch = [
        pltpu.VMEM((512, LATENT), BF16),
        pltpu.VMEM((4, ROPE, BLOCK), BF16),
        pltpu.VMEM((512, DIM), BF16),
        pltpu.VMEM((1, 512), jnp.int32),
        pltpu.VMEM((512, 256), F32),
        pltpu.VMEM((PAIRS * 256, LATENT), BF16),
        pltpu.VMEM((PAIRS, 256, 3 * DIM), BF16),
        pltpu.VMEM((PAIRS, 256, 256), BF16),
        pltpu.VMEM((PAIRS, BLOCK, DIM), BF16),
        pltpu.VMEM((512, PAIRS * 256), BF16),
        pltpu.VMEM((512, DIM), F32),
        pltpu.VMEM((4, BLOCK, LATENT + DIM), F32),
        pltpu.VMEM((3, BLOCK, LATENT + DIM), BF16),
        pltpu.VMEM((3, BLOCK, LATENT + DIM), BF16),
        pltpu.VMEM((256, PAIRS * 256), BF16),
        pltpu.VMEM((2, 256, 256), BF16),
        pltpu.VMEM((PAIRS, 256, 256), F32),
        pltpu.VMEM((PAIRS, 256, 256), F32),
        pltpu.VMEM((PAIRS, 8, 256), F32),
        pltpu.VMEM((PAIRS, 512, 256), BF16),
        pltpu.VMEM((PAIRS, 512, 256), BF16),
        pltpu.VMEM((PAIRS, 2, 4, 4, 16, 256), BF16),
        pltpu.VMEM((PAIRS, 2, 3, 4, 16, 256), BF16),
        pltpu.VMEM((PAIRS, 2, 4, 16, 256), F32),
        pltpu.VMEM((PAIRS, 2, 4, 16, 256), BF16),
        pltpu.VMEM((PAIRS, 2, 3, 16, 256), BF16),
        pltpu.VMEM((2, 2, 4, 4, 16, 256), BF16),
        pltpu.VMEM((PAIRS, 16, LATENT), F32),
        pltpu.VMEM((PAIRS, 16, LATENT), BF16),
        pltpu.VMEM((PAIRS, 16, LATENT), BF16),
        dma((4,)), dma((PAIRS,)), dma((PAIRS,)),
        dma((4 + 2 * CHUNKS,)), dma((4 + 2 * CHUNKS,)), dma((PAIRS,)), dma((PAIRS,)),
        dma((2, PAIRS)), dma((2, PAIRS)), dma((3,)), dma((3,)),
        dma((STEPS, PAIRS)), dma((STEPS, PAIRS)), dma((PAIRS,)), dma((PAIRS,)), dma((2,)), dma((2,)),
    ]
    return pl.pallas_call(
        kernel,
        out_shape=(
            jax.ShapeDtypeStruct((BLOCK, 2048), BF16),
            jax.ShapeDtypeStruct((BLOCK, 1024), BF16),
            jax.ShapeDtypeStruct((BLOCK, LATENT), F32),
            jax.ShapeDtypeStruct((ROPE, BLOCK), F32),
            jax.ShapeDtypeStruct((16, LATENT), F32),
        ),
        in_specs=[hbm] * 7,
        out_specs=(pl.BlockSpec(memory_space=pltpu.VMEM),) * 5,
        scratch_shapes=scratch,
        compiler_params=pltpu.CompilerParams(
            collective_id=0, has_side_effects=True, vmem_limit_bytes=VMEM_BYTES
        ),
        name="latent_attention_grads",
    )(*(pltpu.with_memory_space_constraint(a, pltpu.HBM) for a in arrays))


def write_kernel(count, *refs):
    sources, targets, sems = refs[:count], refs[count:2 * count], refs[2 * count]
    copies = [pltpu.make_async_copy(sources[n], targets[n], sems.at[n]) for n in range(count)]
    for copy in copies:
        copy.start()
    for copy in copies:
        copy.wait()


def write(values):
    count = len(values)
    return pl.pallas_call(
        functools.partial(write_kernel, count),
        out_shape=tuple(jax.ShapeDtypeStruct(value.shape, value.dtype) for value in values),
        in_specs=[pl.BlockSpec(memory_space=pltpu.VMEM)] * count,
        out_specs=(pl.BlockSpec(memory_space=pltpu.HBM),) * count,
        scratch_shapes=[pltpu.SemaphoreType.DMA((count,))],
        name="write_results",
    )(*(pltpu.with_memory_space_constraint(v, pltpu.VMEM) for v in values))


def body(q_nope, q_rope, dout, latent, rope_key, doc_ids, w_up):
    outs = write(fused(
        q_nope[0], q_rope[0], dout[0], latent[0], rope_key[0].T, doc_ids,
        w_up.reshape(2, PAIRS, 2, DIM, LATENT),
    ))
    return (outs[0][None], outs[1][None], outs[2][None], outs[3].T[None], outs[4])


def solution(mesh):
    return jax.shard_map(
        body,
        mesh=mesh,
        in_specs=(
            P("dp", "ctx", None),
            P("dp", "ctx", None),
            P("dp", "ctx", None),
            P("dp", "ctx", None),
            P("dp", "ctx", None),
            P("dp", None),
            P(),
        ),
        out_specs=(
            P("dp", "ctx", None),
            P("dp", "ctx", None),
            P("dp", "ctx", None),
            P("dp", "ctx", None),
            P(("ctx", "dp"), None),
        ),
        check_vma=False,
    )
```
